32 devices in a mesh: groups: 2 (over y), feat: 4 (over z), head: 4 (over x, core).
Axes of the slice: x: 2, y: 2, z: 4, core: 2. Of those that a mesh axis runs over, the one named last changes fastest.
Arguments:
- token_ids: int32 [32], P('groups'), parts along dimension 0, may hold values from 0 to 75967
- embedding: bfloat16 [75968, 5120], P('head', 'feat'), may hold values from -16 to 16
- retained: bfloat16 [2, 32, 8, 8256, 128], P(None, 'groups', 'head', 'feat'), parts along dimension 1, may hold values from -0.29882812 to 0.29882812
- query_weight: bfloat16 [2, 5120, 5120], P(None, 'feat', 'head'), may hold values from -0.078125 to 0.078125
- key_weight: bfloat16 [2, 5120, 1024], P(None, 'feat', 'head'), may hold values from -0.078125 to 0.078125
- value_weight: bfloat16 [2, 5120, 1024], P(None, 'feat', 'head'), may hold values from -0.078125 to 0.078125
- gate_weight: bfloat16 [2, 5120, 8], P(None, 'feat', 'head'), may hold values from -0.078125 to 0.078125
- gate_bias: float32 [2, 8], P(None, 'head'), may hold values from -4 to 3
- norm_gain: float32 [2, 5120], P(None, 'feat'), may hold values from 0.1 to 1.9
- read_gain: float32 [2, 128], replicated, may hold values from 0.1 to 1.9
- out_weight: bfloat16 [2, 5120, 5120], P(None, 'head', 'feat'), may hold values from -0.078125 to 0.078125
Outputs:
- hidden_out: bfloat16 [32, 5120], P('groups', 'feat'), parts along dimension 0
The draws below stay inside these ranges and needn't reach their ends.
There are 2 independent parts, one for each index of `groups`. The reference program is written for one: setup_inputs(seed, part) draws one part's arguments, and reference() takes and returns one part's arrays. A program takes and returns all parts, laid end to end along the dimension named above; an argument that names none is the same for every part. Nothing has to cross between parts.
All inputs are finite; a program needn't handle non-finite values.
Results may differ from the reference program's by a relative error of at most 0.01345.
The reference program's roundings to bfloat16 on the way (of `stream`, `normed` and `mixed`) count: a program that leaves them out, or rounds other values in their place, can miss the bound.
Values may be sent and summed in bfloat16 or wider, within the bound.
No kernel may reach another device: no remote copies, remote signals or barrier semaphores. Data moves between devices by JAX's collectives and lax.ppermute only.
A program may use at most 192 MiB of HBM per device.

```python
import math
import jax
import jax.numpy as jnp
import numpy as np
from jax import lax

D = 5120
QH = 40
KVH = 8
HD = 128
VOCAB = 75968
LAYERS = 2
REQ = 16
FEAT = 8256


def draw_embedding(key, part):
    key_base = jax.random.fold_in(key, 11)
    key_rows = jax.random.fold_in(key, 12)
    column = jnp.arange(D, dtype=jnp.float32) / max(D - 1, 1)
    row_scale = jnp.exp(jax.random.uniform(key_rows, (VOCAB, 1), minval=0.0, maxval=math.log(10.0)))
    rising = jnp.exp(math.log(3.0) * column)
    noise = jax.random.normal(key_base, (VOCAB, D))
    return jnp.clip(0.05 * noise * row_scale * rising, -16.0, 16.0).astype(jnp.bfloat16)


def plant(drawn, own_key, smallest, top_value):
    extent = drawn.shape
    index_at = [jax.random.randint(jax.random.fold_in(own_key, axis), (), 0, extent[axis]) for axis in range(len(extent))]
    drawn = drawn.at[tuple(index_at)].set(smallest)
    longest = extent.index(max(extent))
    index_at[longest] = (index_at[longest] + 1) % extent[longest]
    return drawn.at[tuple(index_at)].set(top_value)


def block_levels(rng, shape, cuts, least, top_value):
    def one(axis_at, parts):
        draws = jax.random.uniform(jax.random.fold_in(jax.random.fold_in(rng, 6), axis_at), (parts,), jnp.float32, least / len(cuts), top_value / len(cuts))
        return jnp.repeat(jnp.exp(draws), shape[axis_at] // parts).reshape((-1,) + (1,) * (len(shape) - axis_at - 1))

    loudness = one(*cuts[0])
    for cut in cuts[1:]:
        loudness = loudness * one(*cut)
    return loudness


def scatter_about(own_key, dims, scale, reach, shards=(), kind=jnp.bfloat16):
    factor_of = block_levels(own_key, dims, shards, -0.22, 0.18) if shards else 1.0
    values = jax.random.normal(own_key, dims, jnp.float32) * scale * factor_of
    return jnp.minimum(jnp.maximum(values, -reach), reach).astype(kind)


def setup_inputs(seed: int = 0, part: int = 0) -> dict:
    key_list = jax.random.split(jax.random.key(seed), 12)
    part_keys = jax.random.split(jax.random.fold_in(key_list[11], part), 12)
    return {
        "token_ids": plant(jax.random.randint(part_keys[0], (REQ,), 0, VOCAB), jax.random.fold_in(part_keys[0], 1), 0, VOCAB - 1).astype(jnp.int32),
        "embedding": draw_embedding(jax.random.fold_in(key_list[11], 71), part),
        "retained": scatter_about(part_keys[2], (LAYERS, REQ, KVH, FEAT, HD), 0.05, 0.29882812, ((2, 4), (3, 4))),
        "query_weight": scatter_about(key_list[3], (LAYERS, D, QH * HD), D ** -0.5, 0.078125, ((1, 4), (2, 4))),
        "key_weight": scatter_about(key_list[4], (LAYERS, D, KVH * HD), D ** -0.5, 0.078125, ((1, 4), (2, 4))),
        "value_weight": scatter_about(key_list[5], (LAYERS, D, KVH * HD), D ** -0.5, 0.078125, ((1, 4), (2, 4))),
        "gate_weight": scatter_about(key_list[6], (LAYERS, D, KVH), D ** -0.5, 0.078125, ((1, 4), (2, 4))),
        "gate_bias": jnp.clip(-4.0 + 7.0 * jax.random.uniform(key_list[7], (LAYERS, KVH), jnp.float32) ** block_levels(key_list[7], (LAYERS, KVH), ((1, 4),), -0.2, 0.2), -4.0, 3.0),
        "norm_gain": jnp.clip(1.0 + 0.18 * jax.random.normal(key_list[8], (LAYERS, D), jnp.float32), 0.1, 1.9),
        "read_gain": jnp.clip(1.0 + 0.18 * jax.random.normal(key_list[9], (LAYERS, HD), jnp.float32), 0.1, 1.9),
        "out_weight": scatter_about(key_list[10], (LAYERS, QH * HD, D), (QH * HD) ** -0.5, 0.078125, ((1, 4), (2, 4))),
    }


def reference(token_ids, embedding, retained, query_weight, key_weight, value_weight, gate_weight, gate_bias, norm_gain, read_gain, out_weight):
    pair_left, pair_right = np.triu_indices(HD)
    pair_left = jnp.asarray(pair_left.astype(np.int32))
    pair_right = jnp.asarray(pair_right.astype(np.int32))
    pair_scale = jnp.where(pair_left == pair_right, 1.0, math.sqrt(2.0)).astype(jnp.float32)
    stream = jnp.take(embedding, token_ids, axis=0)
    for layer_index in range(LAYERS):
        stream_wide = stream.astype(jnp.float32)
        sum_sq = lax.optimization_barrier(jnp.sum(stream_wide * stream_wide, axis=-1, keepdims=True))
        normed = (stream_wide * lax.rsqrt(sum_sq / D + 1e-06) * norm_gain[layer_index]).astype(jnp.bfloat16)
        query = jnp.dot(normed, query_weight[layer_index], preferred_element_type=jnp.float32).astype(jnp.bfloat16)
        query = query.reshape(REQ, KVH, QH // KVH, HD)
        key_rows = jnp.dot(normed, key_weight[layer_index], preferred_element_type=jnp.float32).astype(jnp.bfloat16)
        key_rows = key_rows.reshape(REQ, KVH, HD)
        value_rows = jnp.dot(normed, value_weight[layer_index], preferred_element_type=jnp.float32).astype(jnp.bfloat16)
        value_rows = value_rows.reshape(REQ, KVH, HD)
        gate_logit = jnp.dot(normed, gate_weight[layer_index], preferred_element_type=jnp.float32)
        decay_rate = jnp.exp(-jax.nn.softplus(gate_logit + gate_bias[layer_index]))
        query_wide = query.astype(jnp.float32)
        phi_query = (query_wide[..., pair_left] * query_wide[..., pair_right] * pair_scale).astype(jnp.bfloat16)
        key_wide = key_rows.astype(jnp.float32)
        phi_key = (key_wide[..., pair_left] * key_wide[..., pair_right] * pair_scale / HD).astype(jnp.bfloat16)
        history = jnp.einsum('rhgf,rhfe->rhge', phi_query.astype(jnp.float32), retained[layer_index].astype(jnp.float32))
        cross_term = jnp.einsum('rhgf,rhf->rhg', phi_query.astype(jnp.float32), phi_key.astype(jnp.float32))
        readout = decay_rate[:, :, None, None] * history + cross_term[..., None] * value_rows.astype(jnp.float32)[:, :, None, :]
        scaled = readout * lax.rsqrt(lax.optimization_barrier(jnp.mean(readout * readout, axis=-1, keepdims=True)) + 1e-06) * read_gain[layer_index]
        mixed = scaled.astype(jnp.bfloat16).reshape(REQ, QH * HD)
        branch = jnp.dot(mixed, out_weight[layer_index], preferred_element_type=jnp.float32)
        stream = (stream_wide + branch).astype(jnp.bfloat16)
    return stream
```

```python
import functools
import math

import jax
import jax.numpy as jnp
import numpy as np
from jax import lax
from jax.experimental import pallas as pl
from jax.experimental.pallas import tpu as pltpu
from jax.sharding import PartitionSpec as P

D = 5120
EPS = 1e-6
LANES = 128
SLOTS = 8
ROWS = 16
MIB = 2**20
F32 = jnp.float32
BF16 = jnp.bfloat16

VMEM_SPEC = pl.BlockSpec(memory_space=pltpu.VMEM)
HBM_SPEC = pl.BlockSpec(memory_space=pltpu.HBM)
SMEM_SPEC = pl.BlockSpec(memory_space=pltpu.SMEM)


def params(mib):
    return pltpu.CompilerParams(vmem_limit_bytes=mib * MIB)


def resident(array):
    return pltpu.with_memory_space_constraint(array, pltpu.VMEM)


def off_chip(array):
    return pltpu.with_memory_space_constraint(array, pltpu.HBM)


def exchange(own, wire, axis, size):
    if size > 4:
        return [lax.psum(own.astype(F32), axis)]
    others = [
        lax.ppermute(wire, axis, [(rank, rank ^ step) for rank in range(size)])
        for step in range(1, size)
    ]
    return [own] + others


def split(wide):
    high = wide.astype(BF16)
    return high, (wide - high.astype(F32)).astype(BF16)


def split_dot(wide, weight):
    rows = wide.shape[0]
    out = jnp.dot(jnp.concatenate(split(wide), axis=0), weight, preferred_element_type=F32)
    return out[:rows] + out[rows:]


def add_terms(refs):
    terms = [ref[...].astype(F32) for ref in refs]
    while len(terms) > 1:
        terms = [sum(terms[at : at + 2]) for at in range(0, len(terms), 2)]
    return terms[0]


def pick_kernel(ids_ref, table_ref, out_ref, groups_ref, sems):
    requests = out_ref.shape[0]
    table_rows = table_ref.shape[0]
    row_start = lax.axis_index("head") * table_rows
    row_at = lax.broadcasted_iota(jnp.int32, (requests, requests * ROWS), 0)
    column_at = lax.broadcasted_iota(jnp.int32, (requests, requests * ROWS), 1)
    chosen = jnp.zeros((requests, requests * ROWS), F32)
    copies = []
    for request in range(requests):
        local_id = ids_ref[request] - row_start
        inside = (local_id >= 0) & (local_id < table_rows)
        row = jnp.clip(local_id, 0, table_rows - 1)
        first = pl.multiple_of((row // ROWS) * ROWS, ROWS)
        copy = pltpu.make_async_copy(
            table_ref.at[pl.ds(first, ROWS), :],
            groups_ref.at[pl.ds(request * ROWS, ROWS), :],
            sems.at[request],
        )
        copy.start()
        copies.append(copy)
        place = jnp.where(inside, request * ROWS + row - first, -1)
        chosen = jnp.where((row_at == request) & (column_at == place), 1.0, chosen)
    for copy in copies:
        copy.wait()
    out_ref[...] = jnp.dot(
        chosen.astype(BF16), groups_ref[...], preferred_element_type=F32
    ).astype(BF16)


def pick_rows(token_ids, embedding):
    table_rows, width = embedding.shape
    requests = token_ids.shape[0]
    if table_rows % ROWS:
        local_ids = token_ids - lax.axis_index("head") * table_rows
        inside = (local_ids >= 0) & (local_ids < table_rows)
        picked = jnp.take(embedding, jnp.clip(local_ids, 0, table_rows - 1), axis=0)
        return jnp.where(inside[:, None], picked, jnp.zeros_like(picked))
    return pl.pallas_call(
        pick_kernel,
        out_shape=jax.ShapeDtypeStruct((requests, width), BF16),
        in_specs=[SMEM_SPEC, HBM_SPEC],
        out_specs=VMEM_SPEC,
        scratch_shapes=[
            pltpu.VMEM((requests * ROWS, width), BF16),
            pltpu.SemaphoreType.DMA((requests,)),
        ],
        compiler_params=params(8),
        name="pick_rows",
    )(off_chip(token_ids), off_chip(embedding))


def fetch_kernel(plan, count, *refs):
    sources, outs, sems = refs[:count], refs[count:-1], refs[-1]
    copies = []
    for at, (source, index) in enumerate(plan):
        copy = pltpu.make_async_copy(sources[source].at[index], outs[at], sems.at[at])
        copy.start()
        copies.append(copy)
    for copy in copies:
        copy.wait()


def fetch(sources, plan):
    shapes = []
    for source, index in plan:
        array = sources[source]
        index = index if isinstance(index, tuple) else (index,)
        shape = []
        for at, extent in enumerate(array.shape):
            if at >= len(index):
                shape.append(extent)
            elif isinstance(index[at], slice):
                shape.append(index[at].stop - index[at].start)
        shapes.append(pltpu.VMEM(tuple(shape), array.dtype))
    return pl.pallas_call(
        functools.partial(fetch_kernel, plan, len(sources)),
        out_shape=shapes,
        in_specs=[HBM_SPEC] * len(sources),
        out_specs=[VMEM_SPEC] * len(plan),
        scratch_shapes=[pltpu.SemaphoreType.DMA((len(plan),))],
        compiler_params=params(2),
        name="fetch",
    )(*[off_chip(source) for source in sources])


def select_kernel(pairs_ref, left_ref, right_ref, scale_ref):
    mine = lax.axis_index("feat")
    left = pairs_ref[mine, 0:1, :]
    right = pairs_ref[mine, 1:2, :]
    at = lax.broadcasted_iota(jnp.int32, left_ref.shape, 0)
    at = jnp.where(at >= left_ref.shape[0] // 2, at - left_ref.shape[0] // 2, at)
    left_ref[...] = jnp.where(at == left, 1.0, 0.0).astype(BF16)
    right_ref[...] = jnp.where(at == right, 1.0, 0.0).astype(BF16)
    scale_ref[...] = jnp.where(left == right, 1.0, math.sqrt(2.0)).astype(F32)


def selectors(head_size, block_feat, feat_size):
    pairs = np.stack(np.triu_indices(head_size)).astype(np.int32)
    pairs = pairs.reshape(2, feat_size, block_feat).transpose(1, 0, 2)
    return pl.pallas_call(
        select_kernel,
        out_shape=[
            pltpu.VMEM((2 * head_size, block_feat), BF16),
            pltpu.VMEM((2 * head_size, block_feat), BF16),
            pltpu.VMEM((1, block_feat), F32),
        ],
        in_specs=[VMEM_SPEC],
        out_specs=[VMEM_SPEC] * 3,
        compiler_params=params(8),
        name="selectors",
    )(jnp.asarray(pairs))


def project_kernel(layer, count, carried, *refs):
    terms = refs[carried:count]
    gain_ref, query_ref, key_ref, value_ref, gate_ref = refs[count : count + 5]
    stream_ref, own_ref, wire_ref = refs[count + 5 :]
    stream = add_terms(terms)
    if carried:
        stream = refs[0][...].astype(F32) + stream
    stream = stream.astype(BF16)
    stream_ref[...] = stream
    wide = stream.astype(F32)
    sum_sq = jnp.sum(wide * wide, axis=1, keepdims=True)
    scaled = wide * gain_ref[layer : layer + 1, :]
    start = 0
    for weight_ref in (query_ref, key_ref, value_ref):
        width = weight_ref.shape[2]
        part = split_dot(scaled, weight_ref[layer])
        own_ref[:, start : start + width] = part
        wire_ref[:, start : start + width] = part.astype(BF16)
        start += width
    lane = lax.broadcasted_iota(jnp.int32, (stream.shape[0], LANES), 1)
    half = LANES // 2
    place = jnp.where(lane >= half, lane - half, lane)
    extra = jnp.where(place == 0, sum_sq, 0.0)
    for head in range(gate_ref.shape[1]):
        column = gate_ref[layer, head : head + 1, :].astype(F32)
        gate = jnp.sum(scaled * column, axis=1, keepdims=True)
        extra = jnp.where(place == head + 1, gate, extra)
    own_ref[:, start:] = jnp.where(lane < half, extra, 0.0)
    rounded = extra.astype(BF16).astype(F32)
    wire_ref[:, start:] = jnp.where(lane < half, rounded, extra - rounded).astype(BF16)


def project(layer, carried, terms, norm_gain, weights, gate_weight):
    terms = carried + terms
    requests, width = terms[0].shape
    total = sum(weight.shape[2] for weight in weights) + LANES
    return pl.pallas_call(
        functools.partial(project_kernel, layer, len(terms), len(carried)),
        out_shape=[
            jax.ShapeDtypeStruct((requests, width), BF16),
            jax.ShapeDtypeStruct((requests, total), F32),
            jax.ShapeDtypeStruct((requests, total), BF16),
        ],
        in_specs=[VMEM_SPEC] * (len(terms) + 5),
        out_specs=[VMEM_SPEC] * 3,
        compiler_params=params(8),
        name="project",
    )(*terms, norm_gain, *[resident(weight) for weight in weights], gate_weight)


def read_kernel(layer, sizes, count, held, *refs):
    local_heads, group_size, head_size = sizes
    terms = refs[:count]
    bias_ref, left_ref, right_ref, scale_ref = refs[count : count + 4]
    held_refs = refs[count + 4 : count + 4 + len(held)]
    rest = refs[count + 4 + len(held) :]
    state_ref, own_ref, wire_ref, rows_ref, phi_ref, cross_ref, history_ref, late_ref, sems = rest
    requests = own_ref.shape[0]
    block_feat = phi_ref.shape[2]
    early = sum(held)
    copies = []
    for at in range(requests - early):
        copy = pltpu.make_async_copy(state_ref.at[layer, early + at], late_ref.at[at], sems.at[at])
        copy.start()
        copies.append(copy)

    total = add_terms(terms)
    query_width = local_heads * group_size * head_size
    kv_width = local_heads * head_size
    extra = total[:, query_width + 2 * kv_width :]
    half = LANES // 2
    extra = extra[:, :half] + extra[:, half:]
    inverse = lax.rsqrt(extra[:, 0:1] / D + EPS)
    normed = total[:, : query_width + 2 * kv_width] * inverse

    span = local_heads * SLOTS
    key_slot = group_size
    for head in range(local_heads):
        for slot in range(SLOTS):
            if slot < group_size:
                start = (head * group_size + slot) * head_size
                part = normed[:, start : start + head_size]
            elif slot == key_slot:
                start = query_width + head * head_size
                part = normed[:, start : start + head_size]
            else:
                part = jnp.zeros((requests, head_size), F32)
            rows_ref[pl.ds(head * SLOTS + slot, requests, stride=span), :] = part
    vectors = jnp.concatenate(split(rows_ref[...]), axis=1)

    step = 2 * LANES
    for start in range(0, block_feat, step):
        stop = min(start + step, block_feat)
        left = jnp.dot(vectors, left_ref[:, start:stop], preferred_element_type=F32)
        right = jnp.dot(vectors, right_ref[:, start:stop], preferred_element_type=F32)
        phi = left * right * scale_ref[:, start:stop]
        for part, values in enumerate(split(phi)):
            phi_ref[part, :, start:stop] = values
        wide = phi.reshape(requests * local_heads, SLOTS, stop - start)
        cross = (wide * wide[:, key_slot : key_slot + 1, :]).reshape(-1, stop - start)
        for at in range(0, stop - start, LANES):
            lanes = min(LANES, stop - start - at)
            piece = cross[:, at : at + lanes]
            if start + at == 0:
                cross_ref[:, :lanes] = piece
            else:
                cross_ref[:, :lanes] += piece

    def one_request(request, states):
        mine = slice(request * span, (request + 1) * span)
        rows = jnp.concatenate([phi_ref[0, mine, :], phi_ref[1, mine, :]], axis=0)
        state = jnp.concatenate(states, axis=1) if local_heads > 1 else states[0]
        out = jnp.dot(rows, state, preferred_element_type=F32)
        out = out[:span] + out[span:]
        for head in range(local_heads):
            at = head * SLOTS
            history_ref[request * span + at : request * span + at + SLOTS, :] = out[
                at : at + SLOTS, head * head_size : (head + 1) * head_size
            ]

    request = 0
    for held_ref, many in zip(held_refs, held):
        for at in range(many):
            one_request(request, [held_ref[at, head] for head in range(local_heads)])
            request += 1
    for at, copy in enumerate(copies):
        copy.wait()
        one_request(request, [late_ref[at, head] for head in range(local_heads)])
        request += 1

    for head in range(local_heads):
        logit = extra[:, head + 1 : head + 2] * inverse
        logit = logit + bias_ref[layer : layer + 1, head : head + 1]
        softplus = jnp.maximum(logit, 0.0) + jnp.log(1.0 + jnp.exp(-jnp.abs(logit)))
        decay = jnp.exp(-softplus)
        start = query_width + kv_width + head * head_size
        value = normed[:, start : start + head_size]
        for slot in range(group_size):
            picked = pl.ds(head * SLOTS + slot, requests, stride=span)
            cross = jnp.sum(cross_ref[picked, :], axis=1, keepdims=True) / head_size
            part = decay * history_ref[picked, :] + cross * value
            start = (head * group_size + slot) * head_size
            own_ref[:, start : start + head_size] = part
            wire_ref[:, start : start + head_size] = part.astype(BF16)


def read(layer, sizes, terms, gate_bias, picks, held, retained):
    local_heads, group_size, head_size = sizes
    requests = terms[0].shape[0]
    block_feat = retained.shape[3]
    width = local_heads * group_size * head_size
    counts = tuple(array.shape[0] for array in held)
    late = requests - sum(counts)
    rows = requests * local_heads * SLOTS
    return pl.pallas_call(
        functools.partial(read_kernel, layer, sizes, len(terms), counts),
        out_shape=[
            jax.ShapeDtypeStruct((requests, width), F32),
            jax.ShapeDtypeStruct((requests, width), BF16),
        ],
        in_specs=[VMEM_SPEC] * (len(terms) + 4 + len(held)) + [HBM_SPEC],
        out_specs=[VMEM_SPEC] * 2,
        scratch_shapes=[
            pltpu.VMEM((rows, head_size), F32),
            pltpu.VMEM((2, rows, block_feat), BF16),
            pltpu.VMEM((rows, LANES), F32),
            pltpu.VMEM((rows, head_size), F32),
            pltpu.VMEM((max(late, 1),) + retained.shape[2:], BF16),
            pltpu.SemaphoreType.DMA((max(late, 1),)),
        ],
        compiler_params=params(12),
        name="read",
    )(*terms, gate_bias, *[resident(pick) for pick in picks], *[resident(part) for part in held], off_chip(retained))


def mix_kernel(layer, count, *refs):
    terms = refs[:count]
    gain_ref, weight_ref, wire_ref, mixed_ref = refs[count:]
    head_size = gain_ref.shape[1]
    readout = add_terms(terms)
    gain = gain_ref[layer : layer + 1, :]
    for start in range(0, readout.shape[1], head_size):
        part = readout[:, start : start + head_size]
        mean = jnp.mean(part * part, axis=1, keepdims=True)
        mixed_ref[:, start : start + head_size] = part * lax.rsqrt(mean + EPS) * gain
    wire_ref[...] = split_dot(mixed_ref[...], weight_ref[layer]).astype(wire_ref.dtype)


def mix(layer, terms, read_gain, weight, wire_type):
    requests, rows = terms[0].shape
    return pl.pallas_call(
        functools.partial(mix_kernel, layer, len(terms)),
        out_shape=jax.ShapeDtypeStruct((requests, weight.shape[2]), wire_type),
        in_specs=[VMEM_SPEC] * (len(terms) + 2),
        out_specs=VMEM_SPEC,
        scratch_shapes=[pltpu.VMEM((requests, rows), F32)],
        compiler_params=params(8),
        name="mix",
    )(*terms, read_gain, resident(weight))


def finish_kernel(count, *refs):
    stream = refs[0][...].astype(F32) + add_terms(refs[1:count])
    refs[count][...] = stream.astype(BF16)


def finish(terms):
    return pl.pallas_call(
        functools.partial(finish_kernel, len(terms)),
        out_shape=jax.ShapeDtypeStruct(terms[0].shape, BF16),
        in_specs=[VMEM_SPEC] * len(terms),
        out_specs=VMEM_SPEC,
        compiler_params=params(2),
        name="finish",
    )(*terms)


def body(
    feat_size,
    head_ranks,
    token_ids,
    embedding,
    retained,
    query_weight,
    key_weight,
    value_weight,
    gate_weight,
    gate_bias,
    norm_gain,
    read_gain,
    out_weight,
):
    layer_count, requests, local_heads, block_feat, head_size = retained.shape
    group_size = query_weight.shape[2] // (local_heads * head_size)
    sizes = (local_heads, group_size, head_size)
    weights = (query_weight, key_weight, value_weight)
    gate_rows = gate_weight.transpose(0, 2, 1)
    picks = selectors(head_size, block_feat, feat_size)

    picked = pick_rows(token_ids, embedding)
    stream_terms = exchange(picked, picked, "head", head_ranks)
    stream = None
    for layer in range(layer_count):
        carried = [] if stream is None else [stream]
        stream, own, wire = project(layer, carried, stream_terms, norm_gain, weights, gate_rows)
        terms = exchange(own, wire, "feat", feat_size)
        early = requests * 10 // 16
        held = fetch([retained], ((0, (layer, slice(0, early))),))
        own, wire = read(layer, sizes, terms, gate_bias, picks, held, retained)
        terms = exchange(own, wire, "feat", feat_size)
        wire_type = F32 if head_ranks > 4 else BF16
        wire = mix(layer, terms, read_gain, out_weight, wire_type)
        stream_terms = exchange(wire, wire, "head", head_ranks)
    return finish([stream] + stream_terms)


def solution(mesh):
    return jax.shard_map(
        functools.partial(body, mesh.shape["feat"], mesh.shape["head"]),
        mesh=mesh,
        in_specs=(
            P("groups"),
            P("head", "feat"),
            P(None, "groups", "head", "feat", None),
            P(None, "feat", "head"),
            P(None, "feat", "head"),
            P(None, "feat", "head"),
            P(None, "feat", "head"),
            P(None, "head"),
            P(None, "feat"),
            P(),
            P(None, "head", "feat"),
        ),
        out_specs=P("groups", "feat"),
        check_vma=False,
    )
```

```python
import functools
import math

import jax
import jax.numpy as jnp
import numpy as np
from jax import lax
from jax.experimental import pallas as pl
from jax.experimental.pallas import tpu as pltpu
from jax.sharding import PartitionSpec as P

EPS = 1e-6
LANES = 128
SUBLANES = 8
ROWS = 16
FIRST_LAYER = (0, 7, 9)
LATER_LAYER = (5, 4, 7)
MIB = 2**20
F32 = jnp.float32
BF16 = jnp.bfloat16

VMEM_SPEC = pl.BlockSpec(memory_space=pltpu.VMEM)
ANY_SPEC = pl.BlockSpec(memory_space=pl.ANY)
HBM_SPEC = pl.BlockSpec(memory_space=pltpu.HBM)
SMEM_SPEC = pl.BlockSpec(memory_space=pltpu.SMEM)


def params(mib):
    return pltpu.CompilerParams(vmem_limit_bytes=mib * MIB)


def resident(array):
    return pltpu.with_memory_space_constraint(array, pltpu.VMEM)


def off_chip(array):
    return pltpu.with_memory_space_constraint(array, pltpu.HBM)


def wire_type(size):
    return BF16 if size <= 4 else F32


def exchange(own, wire, axis, size):
    if wire_type(size) == F32:
        return [own.astype(F32) - wire.astype(F32), lax.psum(wire.astype(F32), axis)]
    others = [
        lax.ppermute(wire, axis, [(rank, rank ^ step) for rank in range(size)])
        for step in reversed(range(1, size))
    ]
    return [own] + others


def split(wide):
    high = wide.astype(BF16)
    return high, (wide - high.astype(F32)).astype(BF16)


def split_dot(wide, weight):
    rows = wide.shape[0]
    out = jnp.dot(jnp.concatenate(split(wide), axis=0), weight, preferred_element_type=F32)
    return out[:rows] + out[rows:]


def add_terms(refs):
    terms = [ref[...].astype(F32) for ref in refs]
    while len(terms) > 1:
        terms = [sum(terms[at : at + 2]) for at in range(0, len(terms), 2)]
    return terms[0]


def pick_kernel(ids_ref, table_ref, out_ref, groups_ref, sems):
    requests = out_ref.shape[0]
    table_rows = table_ref.shape[0]
    row_start = lax.axis_index("head") * table_rows
    row_at = lax.broadcasted_iota(jnp.int32, (requests, requests * ROWS), 0)
    column_at = lax.broadcasted_iota(jnp.int32, (requests, requests * ROWS), 1)
    chosen = jnp.zeros((requests, requests * ROWS), F32)
    groups_ref[...] = jnp.zeros_like(groups_ref)
    copies = []
    for request in range(requests):
        local_id = ids_ref[request] - row_start
        inside = (local_id >= 0) & (local_id < table_rows)
        row = jnp.clip(local_id, 0, table_rows - 1)
        first = pl.multiple_of((row // ROWS) * ROWS, ROWS)
        copy = pltpu.make_async_copy(
            table_ref.at[pl.ds(first, ROWS), :],
            groups_ref.at[pl.ds(request * ROWS, ROWS), :],
            sems.at[request],
        )
        pl.when(inside)(copy.start)
        copies.append((inside, copy))
        place = jnp.where(inside, request * ROWS + row - first, -1)
        chosen = jnp.where((row_at == request) & (column_at == place), 1.0, chosen)
    for inside, copy in copies:
        pl.when(inside)(copy.wait)
    out_ref[...] = jnp.dot(
        chosen.astype(BF16), groups_ref[...], preferred_element_type=F32
    ).astype(BF16)


def pick_rows(token_ids, embedding):
    table_rows, width = embedding.shape
    requests = token_ids.shape[0]
    if table_rows % ROWS:
        local_ids = token_ids - lax.axis_index("head") * table_rows
        inside = (local_ids >= 0) & (local_ids < table_rows)
        picked = jnp.take(embedding, jnp.clip(local_ids, 0, table_rows - 1), axis=0)
        return jnp.where(inside[:, None], picked, jnp.zeros_like(picked))
    return pl.pallas_call(
        pick_kernel,
        out_shape=jax.ShapeDtypeStruct((requests, width), BF16),
        in_specs=[SMEM_SPEC, HBM_SPEC],
        out_specs=VMEM_SPEC,
        scratch_shapes=[
            pltpu.VMEM((requests * ROWS, width), BF16),
            pltpu.SemaphoreType.DMA((requests,)),
        ],
        compiler_params=params(8),
        name="pick_rows",
    )(off_chip(token_ids), off_chip(embedding))


def fetch_kernel(plan, count, *refs):
    sources, outs, sems = refs[:count], refs[count:-1], refs[-1]
    copies = []
    for at, (source, index) in enumerate(plan):
        copy = pltpu.make_async_copy(sources[source].at[index], outs[at], sems.at[at])
        copy.start()
        copies.append(copy)
    for copy in copies:
        copy.wait()


def fetch(sources, plan):
    shapes = []
    for source, index in plan:
        array = sources[source]
        index = index if isinstance(index, tuple) else (index,)
        shape = []
        for at, extent in enumerate(array.shape):
            if at >= len(index):
                shape.append(extent)
            elif isinstance(index[at], slice):
                shape.append(index[at].stop - index[at].start)
        shapes.append(pltpu.VMEM(tuple(shape), array.dtype))
    return pl.pallas_call(
        functools.partial(fetch_kernel, plan, len(sources)),
        out_shape=shapes,
        in_specs=[HBM_SPEC] * len(sources),
        out_specs=[VMEM_SPEC] * len(plan),
        scratch_shapes=[pltpu.SemaphoreType.DMA((len(plan),))],
        compiler_params=params(2),
        name="fetch",
    )(*[off_chip(source) for source in sources])


def select_kernel(pairs_ref, left_ref, right_ref, scale_ref):
    mine = lax.axis_index("feat")
    left = pairs_ref[mine, 0:1, :]
    right = pairs_ref[mine, 1:2, :]
    at = lax.broadcasted_iota(jnp.int32, left_ref.shape, 0)
    at = jnp.where(at >= left_ref.shape[0] // 2, at - left_ref.shape[0] // 2, at)
    left_ref[...] = jnp.where(at == left, 1.0, 0.0).astype(BF16)
    right_ref[...] = jnp.where(at == right, 1.0, 0.0).astype(BF16)
    scale_ref[...] = jnp.where(left == right, 1.0, math.sqrt(2.0)).astype(F32)


def selectors(head_size, block_feat, feat_size):
    pairs = np.stack(np.triu_indices(head_size)).astype(np.int32)
    pairs = pairs.reshape(2, feat_size, block_feat).transpose(1, 0, 2)
    return pl.pallas_call(
        select_kernel,
        out_shape=[
            pltpu.VMEM((2 * head_size, block_feat), BF16),
            pltpu.VMEM((2 * head_size, block_feat), BF16),
            pltpu.VMEM((1, block_feat), F32),
        ],
        in_specs=[VMEM_SPEC],
        out_specs=[VMEM_SPEC] * 3,
        compiler_params=params(8),
        name="selectors",
    )(jnp.asarray(pairs))


def project_kernel(layer, count, carried, held, *refs):
    terms = refs[carried:count]
    gain_ref, query_ref, key_ref, value_ref, gate_ref = refs[count : count + 5]
    stream_ref, own_ref, wire_ref = refs[count + 5 + held :]
    stream = add_terms(terms)
    if carried:
        stream = refs[0][...].astype(F32) + stream
    stream = stream.astype(BF16)
    stream_ref[...] = stream
    wide = stream.astype(F32)
    sum_sq = jnp.sum(wide * wide, axis=1, keepdims=True)
    scaled = wide * gain_ref[layer : layer + 1, :]
    start = 0
    for weight_ref in (query_ref, key_ref, value_ref):
        width = weight_ref.shape[2]
        part = split_dot(scaled, weight_ref[layer])
        own_ref[:, start : start + width] = part
        wire_ref[:, start : start + width] = part.astype(wire_ref.dtype)
        start += width
    lane = lax.broadcasted_iota(jnp.int32, (stream.shape[0], LANES), 1)
    half = LANES // 2
    place = jnp.where(lane >= half, lane - half, lane)
    extra = jnp.where(place == 0, sum_sq, 0.0)
    for head in range(gate_ref.shape[1]):
        column = gate_ref[layer, head : head + 1, :].astype(F32)
        gate = jnp.sum(scaled * column, axis=1, keepdims=True)
        extra = jnp.where(place == head + 1, gate, extra)
    own_ref[:, start:] = jnp.where(lane < half, extra, 0.0)
    rounded = extra.astype(BF16).astype(F32)
    wire_ref[:, start:] = jnp.where(lane < half, rounded, extra - rounded).astype(wire_ref.dtype)


def project(layer, carried, wire, terms, norm_gain, weights, gate_weight, held):
    terms = carried + terms
    requests, width = terms[0].shape
    total = sum(weight.shape[2] for weight in weights) + LANES
    return pl.pallas_call(
        functools.partial(project_kernel, layer, len(terms), len(carried), len(held)),
        out_shape=[
            jax.ShapeDtypeStruct((requests, width), BF16),
            jax.ShapeDtypeStruct((requests, total), F32),
            jax.ShapeDtypeStruct((requests, total), wire),
        ],
        in_specs=[VMEM_SPEC] * (len(terms) + 5) + [ANY_SPEC] * len(held),
        out_specs=[VMEM_SPEC] * 3,
        compiler_params=params(8),
        name="project",
    )(
        *terms,
        norm_gain,
        *[resident(weight) for weight in weights],
        gate_weight,
        *[resident(part) for part in held],
    )


def read_kernel(layer, sizes, count, held, *refs):
    local_heads, group_size, slots, head_size, model_width = sizes
    terms = refs[:count]
    bias_ref, left_ref, right_ref, scale_ref = refs[count : count + 4]
    held_refs = refs[count + 4 : count + 4 + len(held)]
    rest = refs[count + 4 + len(held) :]
    own_ref, wire_ref, rows_ref, phi_ref, history_ref = rest
    requests = own_ref.shape[0]
    block_feat = phi_ref.shape[1]
    total = add_terms(terms)
    query_width = local_heads * group_size * head_size
    kv_width = local_heads * head_size
    extra = total[:, query_width + 2 * kv_width :]
    half = LANES // 2
    extra = extra[:, :half] + extra[:, half:]
    inverse = lax.rsqrt(extra[:, 0:1] / model_width + EPS)
    normed = total[:, : query_width + 2 * kv_width] * inverse

    span = local_heads * slots
    for head in range(local_heads):
        for slot in range(slots):
            if slot < group_size:
                start = (head * group_size + slot) * head_size
                part = normed[:, start : start + head_size]
            else:
                part = jnp.zeros((requests, head_size), F32)
            rows_ref[pl.ds(head * slots + slot, requests, stride=span), :] = part
    vectors = jnp.concatenate(split(rows_ref[...]), axis=1)

    step = 2 * LANES
    for start in range(0, block_feat, step):
        stop = min(start + step, block_feat)
        left = jnp.dot(vectors, left_ref[:, start:stop], preferred_element_type=F32)
        right = jnp.dot(vectors, right_ref[:, start:stop], preferred_element_type=F32)
        phi_ref[:, start:stop] = (left * right * scale_ref[:, start:stop]).astype(BF16)

    def one_request(request, states):
        rows = phi_ref[request * span : (request + 1) * span, :]
        state = jnp.concatenate(states, axis=1) if local_heads > 1 else states[0]
        out = jnp.dot(rows, state, preferred_element_type=F32)
        for head in range(local_heads):
            at = head * slots
            history_ref[request * span + at : request * span + at + slots, :] = out[
                at : at + slots, head * head_size : (head + 1) * head_size
            ]

    request = 0
    for held_ref, many in zip(held_refs, held):
        for at in range(many):
            one_request(request, [held_ref[at, head] for head in range(local_heads)])
            request += 1

    for head in range(local_heads):
        logit = extra[:, head + 1 : head + 2] * inverse
        logit = logit + bias_ref[layer : layer + 1, head : head + 1]
        softplus = jnp.maximum(logit, 0.0) + jnp.log(1.0 + jnp.exp(-jnp.abs(logit)))
        decay = jnp.exp(-softplus)
        start = query_width + head * head_size
        key = normed[:, start : start + head_size]
        value = normed[:, start + kv_width : start + kv_width + head_size]
        for slot in range(group_size):
            start = (head * group_size + slot) * head_size
            query = normed[:, start : start + head_size]
            product = jnp.sum(query * key, axis=1, keepdims=True)
            cross = product * product / head_size
            part = decay * history_ref[pl.ds(head * slots + slot, requests, stride=span), :]
            own_ref[:, start : start + head_size] = part + cross * value
            wire_ref[:, start : start + head_size] = part.astype(wire_ref.dtype)


def read(layer, sizes, wire, terms, gate_bias, picks, held):
    local_heads, group_size, slots, head_size, _ = sizes
    requests = terms[0].shape[0]
    block_feat = picks[0].shape[1]
    width = local_heads * group_size * head_size
    counts = tuple(array.shape[0] for array in held)
    rows = requests * local_heads * slots
    return pl.pallas_call(
        functools.partial(read_kernel, layer, sizes, len(terms), counts),
        out_shape=[
            jax.ShapeDtypeStruct((requests, width), F32),
            jax.ShapeDtypeStruct((requests, width), wire),
        ],
        in_specs=[VMEM_SPEC] * (len(terms) + 4 + len(held)),
        out_specs=[VMEM_SPEC] * 2,
        scratch_shapes=[
            pltpu.VMEM((rows, head_size), F32),
            pltpu.VMEM((rows, block_feat), BF16),
            pltpu.VMEM((rows, head_size), F32),
        ],
        compiler_params=params(6),
        name="read",
    )(*terms, gate_bias, *[resident(array) for array in (*picks, *held)])


def mix_kernel(layer, count, held, *refs):
    terms = refs[:count]
    gain_ref, weight_ref = refs[count : count + 2]
    wire_ref, mixed_ref = refs[count + 2 + held :]
    head_size = gain_ref.shape[1]
    readout = add_terms(terms)
    gain = gain_ref[layer : layer + 1, :]
    for start in range(0, readout.shape[1], head_size):
        part = readout[:, start : start + head_size]
        mean = jnp.mean(part * part, axis=1, keepdims=True)
        mixed_ref[:, start : start + head_size] = part * lax.rsqrt(mean + EPS) * gain
    wire_ref[...] = split_dot(mixed_ref[...], weight_ref[layer]).astype(wire_ref.dtype)


def mix(layer, wire, terms, read_gain, weight, held):
    requests, rows = terms[0].shape
    return pl.pallas_call(
        functools.partial(mix_kernel, layer, len(terms), len(held)),
        out_shape=jax.ShapeDtypeStruct((requests, weight.shape[2]), wire),
        in_specs=[VMEM_SPEC] * (len(terms) + 2) + [ANY_SPEC] * len(held),
        out_specs=VMEM_SPEC,
        scratch_shapes=[pltpu.VMEM((requests, rows), F32)],
        compiler_params=params(8),
        name="mix",
    )(*terms, read_gain, resident(weight), *[resident(part) for part in held])


def finish_kernel(count, *refs):
    stream = refs[0][...].astype(F32) + add_terms(refs[1:count])
    refs[count][...] = stream.astype(BF16)


def finish(terms):
    return pl.pallas_call(
        functools.partial(finish_kernel, len(terms)),
        out_shape=jax.ShapeDtypeStruct(terms[0].shape, BF16),
        in_specs=[VMEM_SPEC] * len(terms),
        out_specs=VMEM_SPEC,
        compiler_params=params(2),
        name="finish",
    )(*terms)


def body(
    feat_size,
    head_ranks,
    token_ids,
    embedding,
    retained,
    query_weight,
    key_weight,
    value_weight,
    gate_weight,
    gate_bias,
    norm_gain,
    read_gain,
    out_weight,
):
    layer_count, requests, local_heads, block_feat, head_size = retained.shape
    group_size = query_weight.shape[2] // (local_heads * head_size)
    slots = -(-group_size // SUBLANES) * SUBLANES
    model_width = norm_gain.shape[1] * feat_size
    sizes = (local_heads, group_size, slots, head_size, model_width)
    feat_wire = wire_type(feat_size)
    head_wire = wire_type(head_ranks)
    weights = (query_weight, key_weight, value_weight)
    gate_rows = gate_weight.transpose(0, 2, 1)
    picks = selectors(head_size, block_feat, feat_size)

    def fetch_state(layer, stage):
        shares = LATER_LAYER if layer else FIRST_LAYER
        start = requests * sum(shares[:stage]) // sum(shares)
        stop = requests * sum(shares[: stage + 1]) // sum(shares)
        if layer >= layer_count or start == stop:
            return []
        return list(fetch([retained], ((0, (layer, slice(start, stop))),)))

    picked = pick_rows(token_ids, embedding)
    stream_terms = exchange(picked, picked, "head", head_ranks)
    carried, held = [], []
    for layer in range(layer_count):
        held = held + fetch_state(layer, 1)
        stream, own, wire = project(
            layer, carried, feat_wire, stream_terms, norm_gain, weights, gate_rows, held
        )
        terms = exchange(own, wire, "feat", feat_size)
        held = held + fetch_state(layer, 2)
        own, wire = read(layer, sizes, feat_wire, terms, gate_bias, picks, held)
        terms = exchange(own, wire, "feat", feat_size)
        held = fetch_state(layer + 1, 0)
        wire = mix(layer, head_wire, terms, read_gain, out_weight, held)
        stream_terms = exchange(wire, wire, "head", head_ranks)
        carried = [stream]
    return finish(carried + stream_terms)


def solution(mesh):
    return jax.shard_map(
        functools.partial(body, mesh.shape["feat"], mesh.shape["head"]),
        mesh=mesh,
        in_specs=(
            P("groups"),
            P("head", "feat"),
            P(None, "groups", "head", "feat", None),
            P(None, "feat", "head"),
            P(None, "feat", "head"),
            P(None, "feat", "head"),
            P(None, "feat", "head"),
            P(None, "head"),
            P(None, "feat"),
            P(),
            P(None, "head", "feat"),
        ),
        out_specs=P("groups", "feat"),
        check_vma=False,
    )
```

```python
import functools
import math

import jax
import jax.numpy as jnp
from jax import lax
from jax.experimental import pallas as pl
from jax.experimental.pallas import tpu as pltpu
from jax.sharding import PartitionSpec as P

EPS = 1e-6
LANES = 128
SUBLANES = 8
ROWS = 16
FIRST_LAYER = (0, 6, 10)
LATER_LAYER = (5, 4, 7)
MIB = 2**20
F32 = jnp.float32
BF16 = jnp.bfloat16

VMEM_SPEC = pl.BlockSpec(memory_space=pltpu.VMEM)
ANY_SPEC = pl.BlockSpec(memory_space=pl.ANY)
HBM_SPEC = pl.BlockSpec(memory_space=pltpu.HBM)
SMEM_SPEC = pl.BlockSpec(memory_space=pltpu.SMEM)


def params(mib):
    return pltpu.CompilerParams(vmem_limit_bytes=mib * MIB)


def resident(array):
    return pltpu.with_memory_space_constraint(array, pltpu.VMEM)


def off_chip(array):
    return pltpu.with_memory_space_constraint(array, pltpu.HBM)


def wire_type(size):
    return BF16 if size <= 4 else F32


def steps_of(size):
    return tuple(reversed(range(1, size))) if size <= 4 else ()


def exchange(own, wires, axis, size):
    steps = steps_of(size)
    if not steps:
        (wire,) = wires
        return [own.astype(F32) - wire.astype(F32), lax.psum(wire.astype(F32), axis)]
    if len(wires) == 1:
        wires = wires * len(steps)
    return [own] + [
        lax.ppermute(wire, axis, [(rank, rank ^ step) for rank in range(size)])
        for wire, step in zip(wires, steps)
    ]


def own_rows(array, share, mine):
    rows = array[:share]
    for block in range(1, array.shape[0] // share):
        rows = jnp.where(mine == block, array[block * share : (block + 1) * share], rows)
    return rows


def split(wide):
    high = wide.astype(BF16)
    return high, (wide - high.astype(F32)).astype(BF16)


def split_dot(wide, weight):
    rows = wide.shape[0]
    out = jnp.dot(jnp.concatenate(split(wide), axis=0), weight, preferred_element_type=F32)
    return out[:rows] + out[rows:]


def add_terms(refs):
    terms = [ref[...].astype(F32) for ref in refs]
    while len(terms) > 1:
        terms = [sum(terms[at : at + 2]) for at in range(0, len(terms), 2)]
    return terms[0]


def make_selectors(left_ref, right_ref, scale_ref):
    depth, block_feat = left_ref.shape
    size = depth // 2

    def first_of(row):
        return row * size - row * (row - 1) // 2

    column = lax.broadcasted_iota(jnp.int32, (1, block_feat), 1)
    feature = lax.axis_index("feat") * block_feat + column
    reach = 2 * size + 1
    root = jnp.sqrt((reach * reach - 8 * feature).astype(F32))
    left = ((reach - root) * 0.5).astype(jnp.int32)
    left = jnp.where(first_of(left) > feature, left - 1, left)
    left = jnp.where(first_of(left + 1) <= feature, left + 1, left)
    right = feature - first_of(left) + left
    at = lax.broadcasted_iota(jnp.int32, left_ref.shape, 0)
    at = jnp.where(at >= size, at - size, at)
    left_ref[...] = jnp.where(at == left, 1.0, 0.0).astype(BF16)
    right_ref[...] = jnp.where(at == right, 1.0, 0.0).astype(BF16)
    scale_ref[...] = jnp.where(left == right, 1.0, math.sqrt(2.0)).astype(F32)


def pick_kernel(ids_ref, table_ref, out_ref, left_ref, right_ref, scale_ref, groups_ref, sems):
    requests = out_ref.shape[0]
    table_rows = table_ref.shape[0]
    row_start = lax.axis_index("head") * table_rows
    row_at = lax.broadcasted_iota(jnp.int32, (requests, requests * ROWS), 0)
    column_at = lax.broadcasted_iota(jnp.int32, (requests, requests * ROWS), 1)
    chosen = jnp.zeros((requests, requests * ROWS), F32)
    groups_ref[...] = jnp.zeros_like(groups_ref)
    copies = []
    for request in range(requests):
        local_id = ids_ref[request] - row_start
        inside = (local_id >= 0) & (local_id < table_rows)
        row = jnp.clip(local_id, 0, table_rows - 1)
        first = pl.multiple_of((row // ROWS) * ROWS, ROWS)
        copy = pltpu.make_async_copy(
            table_ref.at[pl.ds(first, ROWS), :],
            groups_ref.at[pl.ds(request * ROWS, ROWS), :],
            sems.at[request],
        )
        pl.when(inside)(copy.start)
        copies.append((inside, copy))
        place = jnp.where(inside, request * ROWS + row - first, -1)
        chosen = jnp.where((row_at == request) & (column_at == place), 1.0, chosen)
    make_selectors(left_ref, right_ref, scale_ref)
    for inside, copy in copies:
        pl.when(inside)(copy.wait)
    out_ref[...] = jnp.dot(
        chosen.astype(BF16), groups_ref[...], preferred_element_type=F32
    ).astype(BF16)


def pick_rows(token_ids, embedding, head_size, block_feat):
    table_rows, width = embedding.shape
    requests = token_ids.shape[0]
    picks = [
        pltpu.VMEM((2 * head_size, block_feat), BF16),
        pltpu.VMEM((2 * head_size, block_feat), BF16),
        pltpu.VMEM((1, block_feat), F32),
    ]
    if table_rows % ROWS:
        picks = pl.pallas_call(
            make_selectors,
            out_shape=picks,
            out_specs=[VMEM_SPEC] * 3,
            compiler_params=params(8),
            name="selectors",
        )()
        local_ids = token_ids - lax.axis_index("head") * table_rows
        inside = (local_ids >= 0) & (local_ids < table_rows)
        picked = jnp.take(embedding, jnp.clip(local_ids, 0, table_rows - 1), axis=0)
        return jnp.where(inside[:, None], picked, jnp.zeros_like(picked)), picks
    picked, *picks = pl.pallas_call(
        pick_kernel,
        out_shape=[jax.ShapeDtypeStruct((requests, width), BF16)] + picks,
        in_specs=[SMEM_SPEC, HBM_SPEC],
        out_specs=[VMEM_SPEC] * 4,
        scratch_shapes=[
            pltpu.VMEM((requests * ROWS, width), BF16),
            pltpu.SemaphoreType.DMA((requests,)),
        ],
        compiler_params=params(8),
        name="pick_rows",
    )(off_chip(token_ids), off_chip(embedding))
    return picked, picks


def fetch_kernel(plan, count, *refs):
    sources, outs, sems = refs[:count], refs[count:-1], refs[-1]
    copies = []
    for at, (source, index) in enumerate(plan):
        copy = pltpu.make_async_copy(sources[source].at[index], outs[at], sems.at[at])
        copy.start()
        copies.append(copy)
    for copy in copies:
        copy.wait()


def fetch(sources, plan):
    shapes = []
    for source, index in plan:
        array = sources[source]
        index = index if isinstance(index, tuple) else (index,)
        shape = []
        for at, extent in enumerate(array.shape):
            if at >= len(index):
                shape.append(extent)
            elif isinstance(index[at], slice):
                shape.append(index[at].stop - index[at].start)
        shapes.append(pltpu.VMEM(tuple(shape), array.dtype))
    return pl.pallas_call(
        functools.partial(fetch_kernel, plan, len(sources)),
        out_shape=shapes,
        in_specs=[HBM_SPEC] * len(sources),
        out_specs=[VMEM_SPEC] * len(plan),
        scratch_shapes=[pltpu.SemaphoreType.DMA((len(plan),))],
        compiler_params=params(2),
        name="fetch",
    )(*[off_chip(source) for source in sources])


def project_kernel(layer, count, carried, held, steps, *refs):
    terms = refs[carried:count]
    gain_ref, query_ref, key_ref, value_ref, gate_ref = refs[count : count + 5]
    stream_ref, own_ref, *wire_refs = refs[count + 5 + held :]
    stream = add_terms(terms)
    if carried:
        stream = refs[0][...].astype(F32) + stream
    stream = stream.astype(BF16)
    stream_ref[...] = stream
    wide = stream.astype(F32)
    sum_sq = jnp.sum(wide * wide, axis=1, keepdims=True)
    scaled = wide * gain_ref[layer : layer + 1, :]
    parts = [
        split_dot(scaled, weight_ref[layer]) for weight_ref in (query_ref, key_ref, value_ref)
    ]
    requests = stream.shape[0]
    lane = lax.broadcasted_iota(jnp.int32, (requests, LANES), 1)
    half = LANES // 2
    place = jnp.where(lane >= half, lane - half, lane)
    extra = jnp.where(place == 0, sum_sq, 0.0)
    for head in range(gate_ref.shape[1]):
        column = gate_ref[layer, head : head + 1, :].astype(F32)
        gate = jnp.sum(scaled * column, axis=1, keepdims=True)
        extra = jnp.where(place == head + 1, gate, extra)
    rounded = extra.astype(BF16).astype(F32)
    sent = jnp.where(lane < half, rounded, extra - rounded)
    kept = jnp.where(lane < half, extra, 0.0)
    start = 0
    for part, other in zip((parts[0], kept, *parts[1:]), (parts[0], sent, *parts[1:])):
        stop = start + part.shape[1]
        own_ref[:, start:stop] = part
        for wire_ref in wire_refs:
            if stop <= wire_ref.shape[1]:
                wire_ref[:, start:stop] = other.astype(wire_ref.dtype)
        start = stop
    for step, wire_ref in zip(steps, wire_refs):
        share = requests // (len(steps) + 1)
        partner = lax.axis_index("feat") ^ step
        packed = [
            own_rows(part[:, at : at + LANES], share, partner)
            for part in parts[1:]
            for at in range(0, part.shape[1], LANES)
        ]
        wire_ref[:, -LANES:] = jnp.concatenate(packed, axis=0).astype(wire_ref.dtype)


def packs(requests, weights, size):
    blocks = sum(weight.shape[2] for weight in weights[1:]) // LANES
    return len(steps_of(size)) > 0 and blocks == size and requests % size == 0


def project(layer, carried, size, terms, norm_gain, weights, gate_weight, held):
    terms = carried + terms
    requests, width = terms[0].shape
    query_width = weights[0].shape[2]
    total = sum(weight.shape[2] for weight in weights) + LANES
    if packs(requests, weights, size):
        steps, sent = steps_of(size), query_width + 2 * LANES
    else:
        steps, sent = (), total
    wires = [jax.ShapeDtypeStruct((requests, sent), wire_type(size))] * max(len(steps), 1)
    stream, own, *wires = pl.pallas_call(
        functools.partial(project_kernel, layer, len(terms), len(carried), len(held), steps),
        out_shape=[
            jax.ShapeDtypeStruct((requests, width), BF16),
            jax.ShapeDtypeStruct((requests, total), F32),
        ]
        + wires,
        in_specs=[VMEM_SPEC] * (len(terms) + 5) + [ANY_SPEC] * len(held),
        out_specs=[VMEM_SPEC] * (2 + len(wires)),
        compiler_params=params(8),
        name="project",
    )(
        *terms,
        norm_gain,
        *[resident(weight) for weight in weights],
        gate_weight,
        *[resident(part) for part in held],
    )
    return stream, own, wires


def read_kernel(layer, sizes, count, held, *refs):
    local_heads, group_size, slots, head_size, stream_width, model_width = sizes
    terms = refs[:count]
    bias_ref, left_ref, right_ref, scale_ref = refs[count : count + 4]
    held_refs = refs[count + 4 : count + 4 + len(held)]
    rest = refs[count + 4 + len(held) :]
    own_ref, wire_ref, rows_ref, phi_ref, history_ref = rest
    requests = own_ref.shape[0]
    block_feat = phi_ref.shape[1]
    query_width = local_heads * group_size * head_size
    kv_width = local_heads * head_size
    own, others = terms[0], terms[1:]
    common = query_width + LANES
    total = add_terms([ref.at[:, :common] for ref in terms])
    extra = total[:, query_width:]
    half = LANES // 2
    extra = extra[:, :half] + extra[:, half:]
    inverse = lax.rsqrt(extra[:, 0:1] / model_width + EPS)
    queries = total[:, :query_width] * inverse

    feat_size = model_width // stream_width
    share = requests // feat_size
    mine = lax.axis_index("feat")
    if others[0].shape[1] == own.shape[1]:
        pairs = add_terms([ref.at[:, common:] for ref in terms])
        pairs = own_rows(pairs, share, mine)
    else:
        packed = add_terms([ref.at[:, common:] for ref in others])
        pairs = own_rows(own[:, common:], share, mine) + jnp.concatenate(
            [packed[at : at + share] for at in range(0, requests, share)], axis=1
        )
    pairs = jnp.concatenate([pairs] * feat_size, axis=0) * inverse
    block = lax.broadcasted_iota(jnp.int32, (requests, 1), 0) // share
    pairs = jnp.where(block == mine, pairs, 0.0)

    span = local_heads * slots
    for head in range(local_heads):
        for slot in range(slots):
            if slot < group_size:
                start = (head * group_size + slot) * head_size
                part = queries[:, start : start + head_size]
            else:
                part = jnp.zeros((requests, head_size), F32)
            rows_ref[pl.ds(head * slots + slot, requests, stride=span), :] = part
    vectors = jnp.concatenate(split(rows_ref[...]), axis=1)

    step = 2 * LANES
    for start in range(0, block_feat, step):
        stop = min(start + step, block_feat)
        left = jnp.dot(vectors, left_ref[:, start:stop], preferred_element_type=F32)
        right = jnp.dot(vectors, right_ref[:, start:stop], preferred_element_type=F32)
        phi_ref[:, start:stop] = (left * right * scale_ref[:, start:stop]).astype(BF16)

    def one_request(request, states):
        rows = phi_ref[request * span : (request + 1) * span, :]
        state = jnp.concatenate(states, axis=1) if local_heads > 1 else states[0]
        out = jnp.dot(rows, state, preferred_element_type=F32)
        for head in range(local_heads):
            at = head * slots
            history_ref[request * span + at : request * span + at + slots, :] = out[
                at : at + slots, head * head_size : (head + 1) * head_size
            ]

    request = 0
    for held_ref, many in zip(held_refs, held):
        for at in range(many):
            one_request(request, [held_ref[at, head] for head in range(local_heads)])
            request += 1

    for head in range(local_heads):
        logit = extra[:, head + 1 : head + 2] * inverse
        logit = logit + bias_ref[layer : layer + 1, head : head + 1]
        softplus = jnp.maximum(logit, 0.0) + jnp.log(1.0 + jnp.exp(-jnp.abs(logit)))
        decay = jnp.exp(-softplus)
        start = head * head_size
        key = pairs[:, start : start + head_size]
        value = pairs[:, start + kv_width : start + kv_width + head_size]
        for slot in range(group_size):
            start = (head * group_size + slot) * head_size
            query = queries[:, start : start + head_size]
            product = jnp.sum(query * key, axis=1, keepdims=True)
            cross = product * product / head_size
            part = decay * history_ref[pl.ds(head * slots + slot, requests, stride=span), :]
            part = part + cross * value
            own_ref[:, start : start + head_size] = part
            wire_ref[:, start : start + head_size] = part.astype(wire_ref.dtype)


def read(layer, sizes, wire, terms, gate_bias, picks, held):
    local_heads, group_size, slots, head_size, _, _ = sizes
    requests = terms[0].shape[0]
    block_feat = picks[0].shape[1]
    width = local_heads * group_size * head_size
    counts = tuple(array.shape[0] for array in held)
    rows = requests * local_heads * slots
    return pl.pallas_call(
        functools.partial(read_kernel, layer, sizes, len(terms), counts),
        out_shape=[
            jax.ShapeDtypeStruct((requests, width), F32),
            jax.ShapeDtypeStruct((requests, width), wire),
        ],
        in_specs=[VMEM_SPEC] * (len(terms) + 4 + len(held)),
        out_specs=[VMEM_SPEC] * 2,
        scratch_shapes=[
            pltpu.VMEM((rows, head_size), F32),
            pltpu.VMEM((rows, block_feat), BF16),
            pltpu.VMEM((rows, head_size), F32),
        ],
        compiler_params=params(6),
        name="read",
    )(*terms, gate_bias, *[resident(array) for array in (*picks, *held)])


def mix_kernel(layer, count, held, *refs):
    terms = refs[:count]
    gain_ref, weight_ref = refs[count : count + 2]
    wire_ref, mixed_ref = refs[count + 2 + held :]
    head_size = gain_ref.shape[1]
    readout = add_terms(terms)
    gain = gain_ref[layer : layer + 1, :]
    for start in range(0, readout.shape[1], head_size):
        part = readout[:, start : start + head_size]
        mean = jnp.mean(part * part, axis=1, keepdims=True)
        mixed_ref[:, start : start + head_size] = part * lax.rsqrt(mean + EPS) * gain
    wire_ref[...] = split_dot(mixed_ref[...], weight_ref[layer]).astype(wire_ref.dtype)


def mix(layer, wire, terms, read_gain, weight, held):
    requests, rows = terms[0].shape
    return pl.pallas_call(
        functools.partial(mix_kernel, layer, len(terms), len(held)),
        out_shape=jax.ShapeDtypeStruct((requests, weight.shape[2]), wire),
        in_specs=[VMEM_SPEC] * (len(terms) + 2) + [ANY_SPEC] * len(held),
        out_specs=VMEM_SPEC,
        scratch_shapes=[pltpu.VMEM((requests, rows), F32)],
        compiler_params=params(8),
        name="mix",
    )(*terms, read_gain, resident(weight), *[resident(part) for part in held])


def finish_kernel(count, *refs):
    stream = refs[0][...].astype(F32) + add_terms(refs[1:count])
    refs[count][...] = stream.astype(BF16)


def finish(terms):
    return pl.pallas_call(
        functools.partial(finish_kernel, len(terms)),
        out_shape=jax.ShapeDtypeStruct(terms[0].shape, BF16),
        in_specs=[VMEM_SPEC] * len(terms),
        out_specs=VMEM_SPEC,
        compiler_params=params(2),
        name="finish",
    )(*terms)


def body(
    feat_size,
    head_ranks,
    token_ids,
    embedding,
    retained,
    query_weight,
    key_weight,
    value_weight,
    gate_weight,
    gate_bias,
    norm_gain,
    read_gain,
    out_weight,
):
    layer_count, requests, local_heads, block_feat, head_size = retained.shape
    group_size = query_weight.shape[2] // (local_heads * head_size)
    slots = -(-group_size // SUBLANES) * SUBLANES
    stream_width = norm_gain.shape[1]
    model_width = stream_width * feat_size
    sizes = (local_heads, group_size, slots, head_size, stream_width, model_width)
    feat_wire = wire_type(feat_size)
    head_wire = wire_type(head_ranks)
    weights = (query_weight, key_weight, value_weight)
    gate_rows = gate_weight.transpose(0, 2, 1)

    def fetch_state(layer, stage):
        shares = LATER_LAYER if layer else FIRST_LAYER
        start = requests * sum(shares[:stage]) // sum(shares)
        stop = requests * sum(shares[: stage + 1]) // sum(shares)
        if layer >= layer_count or start == stop:
            return []
        return list(fetch([retained], ((0, (layer, slice(start, stop))),)))

    picked, picks = pick_rows(token_ids, embedding, head_size, block_feat)
    stream_terms = exchange(picked, [picked], "head", head_ranks)
    carried, held = [], []
    for layer in range(layer_count):
        held = held + fetch_state(layer, 1)
        stream, own, wires = project(
            layer, carried, feat_size, stream_terms, norm_gain, weights, gate_rows, held
        )
        terms = exchange(own, wires, "feat", feat_size)
        held = held + fetch_state(layer, 2)
        own, wire = read(layer, sizes, feat_wire, terms, gate_bias, picks, held)
        terms = exchange(own, [wire], "feat", feat_size)
        held = fetch_state(layer + 1, 0)
        wire = mix(layer, head_wire, terms, read_gain, out_weight, held)
        stream_terms = exchange(wire, [wire], "head", head_ranks)
        carried = [stream]
    return finish(carried + stream_terms)


def solution(mesh):
    return jax.shard_map(
        functools.partial(body, mesh.shape["feat"], mesh.shape["head"]),
        mesh=mesh,
        in_specs=(
            P("groups"),
            P("head", "feat"),
            P(None, "groups", "head", "feat", None),
            P(None, "feat", "head"),
            P(None, "feat", "head"),
            P(None, "feat", "head"),
            P(None, "feat", "head"),
            P(None, "head"),
            P(None, "feat"),
            P(),
            P(None, "head", "feat"),
        ),
        out_specs=P("groups", "feat"),
        check_vma=False,
    )
```

```python
import functools
import math

import jax
import jax.numpy as jnp
from jax import lax
from jax.experimental import pallas as pl
from jax.experimental.pallas import tpu as pltpu
from jax.sharding import PartitionSpec as P

EPS = 1e-6
LANES = 128
SUBLANES = 8
ROWS = 16
FIRST_LAYER = (0, 4, 8, 4)
LATER_LAYER = (5, 4, 7, 0)
MIB = 2**20
F32 = jnp.float32
BF16 = jnp.bfloat16

VMEM_SPEC = pl.BlockSpec(memory_space=pltpu.VMEM)
ANY_SPEC = pl.BlockSpec(memory_space=pl.ANY)
HBM_SPEC = pl.BlockSpec(memory_space=pltpu.HBM)
SMEM_SPEC = pl.BlockSpec(memory_space=pltpu.SMEM)


def params(mib):
    return pltpu.CompilerParams(vmem_limit_bytes=mib * MIB)


def resident(array):
    return pltpu.with_memory_space_constraint(array, pltpu.VMEM)


def off_chip(array):
    return pltpu.with_memory_space_constraint(array, pltpu.HBM)


def wire_type(size):
    return BF16 if size <= 4 else F32


def steps_of(size, axis):
    if size > 4:
        return ()
    order = (2, 3, 1) if axis == "feat" else (3, 2, 1)
    return tuple(step for step in order if step < size)


def exchange(own, wires, axis, size):
    steps = steps_of(size, axis)
    if not steps:
        (wire,) = wires
        return [own.astype(F32) - wire.astype(F32), lax.psum(wire.astype(F32), axis)]
    if len(wires) == 1:
        wires = wires * len(steps)
    return [own] + [
        lax.ppermute(wire, axis, [(rank, rank ^ step) for rank in range(size)])
        for wire, step in zip(wires, steps)
    ]


def own_rows(array, share, mine):
    rows = array[:share]
    for block in range(1, array.shape[0] // share):
        rows = jnp.where(mine == block, array[block * share : (block + 1) * share], rows)
    return rows


def split(wide):
    high = wide.astype(BF16)
    return high, (wide - high.astype(F32)).astype(BF16)


def split_dot(wide, weight):
    rows = wide.shape[0]
    out = jnp.dot(jnp.concatenate(split(wide), axis=0), weight, preferred_element_type=F32)
    return out[:rows] + out[rows:]


def add_terms(refs):
    terms = [ref[...].astype(F32) for ref in refs]
    while len(terms) > 1:
        terms = [sum(terms[at : at + 2]) for at in range(0, len(terms), 2)]
    return terms[0]


def make_selectors(left_ref, right_ref, scale_ref):
    depth, block_feat = left_ref.shape
    size = depth // 2

    def first_of(row):
        return row * size - row * (row - 1) // 2

    column = lax.broadcasted_iota(jnp.int32, (1, block_feat), 1)
    feature = lax.axis_index("feat") * block_feat + column
    reach = 2 * size + 1
    root = jnp.sqrt((reach * reach - 8 * feature).astype(F32))
    left = ((reach - root) * 0.5).astype(jnp.int32)
    left = jnp.where(first_of(left) > feature, left - 1, left)
    left = jnp.where(first_of(left + 1) <= feature, left + 1, left)
    right = feature - first_of(left) + left
    at = lax.broadcasted_iota(jnp.int32, left_ref.shape, 0)
    at = jnp.where(at >= size, at - size, at)
    left_ref[...] = jnp.where(at == left, 1.0, 0.0).astype(BF16)
    right_ref[...] = jnp.where(at == right, 1.0, 0.0).astype(BF16)
    scale_ref[...] = jnp.where(left == right, 1.0, math.sqrt(2.0)).astype(F32)


def pick_kernel(ids_ref, table_ref, out_ref, left_ref, right_ref, scale_ref, groups_ref, sems):
    requests = out_ref.shape[0]
    table_rows = table_ref.shape[0]
    row_start = lax.axis_index("head") * table_rows
    row_at = lax.broadcasted_iota(jnp.int32, (requests, requests * ROWS), 0)
    column_at = lax.broadcasted_iota(jnp.int32, (requests, requests * ROWS), 1)
    chosen = jnp.zeros((requests, requests * ROWS), F32)
    groups_ref[...] = jnp.zeros_like(groups_ref)
    copies = []
    for request in range(requests):
        local_id = ids_ref[request] - row_start
        inside = (local_id >= 0) & (local_id < table_rows)
        row = jnp.clip(local_id, 0, table_rows - 1)
        first = pl.multiple_of((row // ROWS) * ROWS, ROWS)
        copy = pltpu.make_async_copy(
            table_ref.at[pl.ds(first, ROWS), :],
            groups_ref.at[pl.ds(request * ROWS, ROWS), :],
            sems.at[request],
        )
        pl.when(inside)(copy.start)
        copies.append((inside, copy))
        place = jnp.where(inside, request * ROWS + row - first, -1)
        chosen = jnp.where((row_at == request) & (column_at == place), 1.0, chosen)
    make_selectors(left_ref, right_ref, scale_ref)
    for inside, copy in copies:
        pl.when(inside)(copy.wait)
    out_ref[...] = jnp.dot(
        chosen.astype(BF16), groups_ref[...], preferred_element_type=F32
    ).astype(BF16)


def pick_rows(token_ids, embedding, head_size, block_feat):
    table_rows, width = embedding.shape
    requests = token_ids.shape[0]
    picks = [
        pltpu.VMEM((2 * head_size, block_feat), BF16),
        pltpu.VMEM((2 * head_size, block_feat), BF16),
        pltpu.VMEM((1, block_feat), F32),
    ]
    if table_rows % ROWS:
        picks = pl.pallas_call(
            make_selectors,
            out_shape=picks,
            out_specs=[VMEM_SPEC] * 3,
            compiler_params=params(8),
            name="selectors",
        )()
        local_ids = token_ids - lax.axis_index("head") * table_rows
        inside = (local_ids >= 0) & (local_ids < table_rows)
        picked = jnp.take(embedding, jnp.clip(local_ids, 0, table_rows - 1), axis=0)
        return jnp.where(inside[:, None], picked, jnp.zeros_like(picked)), picks
    picked, *picks = pl.pallas_call(
        pick_kernel,
        out_shape=[jax.ShapeDtypeStruct((requests, width), BF16)] + picks,
        in_specs=[SMEM_SPEC, HBM_SPEC],
        out_specs=[VMEM_SPEC] * 4,
        scratch_shapes=[
            pltpu.VMEM((requests * ROWS, width), BF16),
            pltpu.SemaphoreType.DMA((requests,)),
        ],
        compiler_params=params(8),
        name="pick_rows",
    )(off_chip(token_ids), off_chip(embedding))
    return picked, picks


def fetch_kernel(plan, count, *refs):
    sources, outs, sems = refs[:count], refs[count:-1], refs[-1]
    copies = []
    for at, (source, index) in enumerate(plan):
        copy = pltpu.make_async_copy(sources[source].at[index], outs[at], sems.at[at])
        copy.start()
        copies.append(copy)
    for copy in copies:
        copy.wait()


def fetch(sources, plan):
    shapes = []
    for source, index in plan:
        array = sources[source]
        index = index if isinstance(index, tuple) else (index,)
        shape = []
        for at, extent in enumerate(array.shape):
            if at >= len(index):
                shape.append(extent)
            elif isinstance(index[at], slice):
                shape.append(index[at].stop - index[at].start)
        shapes.append(pltpu.VMEM(tuple(shape), array.dtype))
    return pl.pallas_call(
        functools.partial(fetch_kernel, plan, len(sources)),
        out_shape=shapes,
        in_specs=[HBM_SPEC] * len(sources),
        out_specs=[VMEM_SPEC] * len(plan),
        scratch_shapes=[pltpu.SemaphoreType.DMA((len(plan),))],
        compiler_params=params(2),
        name="fetch",
    )(*[off_chip(source) for source in sources])


def project_kernel(layer, count, carried, held, steps, *refs):
    terms = refs[carried:count]
    gain_ref, query_ref, key_ref, value_ref, gate_ref = refs[count : count + 5]
    stream_ref, own_ref, *wire_refs = refs[count + 5 + held :]
    stream = add_terms(terms)
    if carried:
        stream = refs[0][...].astype(F32) + stream
    stream = stream.astype(BF16)
    stream_ref[...] = stream
    wide = stream.astype(F32)
    sum_sq = jnp.sum(wide * wide, axis=1, keepdims=True)
    scaled = wide * gain_ref[layer : layer + 1, :]
    parts = [
        split_dot(scaled, weight_ref[layer]) for weight_ref in (query_ref, key_ref, value_ref)
    ]
    requests = stream.shape[0]
    lane = lax.broadcasted_iota(jnp.int32, (requests, LANES), 1)
    half = LANES // 2
    place = jnp.where(lane >= half, lane - half, lane)
    extra = jnp.where(place == 0, sum_sq, 0.0)
    for head in range(gate_ref.shape[1]):
        column = gate_ref[layer, head : head + 1, :].astype(F32)
        gate = jnp.sum(scaled * column, axis=1, keepdims=True)
        extra = jnp.where(place == head + 1, gate, extra)
    rounded = extra.astype(BF16).astype(F32)
    sent = jnp.where(lane < half, rounded, extra - rounded)
    kept = jnp.where(lane < half, extra, 0.0)
    start = 0
    for part, other in zip((parts[0], kept, *parts[1:]), (parts[0], sent, *parts[1:])):
        stop = start + part.shape[1]
        own_ref[:, start:stop] = part
        for wire_ref in wire_refs:
            if stop <= wire_ref.shape[1]:
                wire_ref[:, start:stop] = other.astype(wire_ref.dtype)
        start = stop
    for step, wire_ref in zip(steps, wire_refs):
        share = requests // (len(steps) + 1)
        partner = lax.axis_index("feat") ^ step
        packed = [
            own_rows(part[:, at : at + LANES], share, partner)
            for part in parts[1:]
            for at in range(0, part.shape[1], LANES)
        ]
        wire_ref[:, -LANES:] = jnp.concatenate(packed, axis=0).astype(wire_ref.dtype)


def packs(requests, weights, size):
    blocks = sum(weight.shape[2] for weight in weights[1:]) // LANES
    return len(steps_of(size, "feat")) > 0 and blocks == size and requests % size == 0


def project(layer, carried, size, terms, norm_gain, weights, gate_weight, held):
    terms = carried + terms
    requests, width = terms[0].shape
    query_width = weights[0].shape[2]
    total = sum(weight.shape[2] for weight in weights) + LANES
    if packs(requests, weights, size):
        steps, sent = steps_of(size, "feat"), query_width + 2 * LANES
    else:
        steps, sent = (), total
    wires = [jax.ShapeDtypeStruct((requests, sent), wire_type(size))] * max(len(steps), 1)
    stream, own, *wires = pl.pallas_call(
        functools.partial(project_kernel, layer, len(terms), len(carried), len(held), steps),
        out_shape=[
            jax.ShapeDtypeStruct((requests, width), BF16),
            jax.ShapeDtypeStruct((requests, total), F32),
        ]
        + wires,
        in_specs=[VMEM_SPEC] * (len(terms) + 5) + [ANY_SPEC] * len(held),
        out_specs=[VMEM_SPEC] * (2 + len(wires)),
        compiler_params=params(8),
        name="project",
    )(
        *terms,
        norm_gain,
        *[resident(weight) for weight in weights],
        gate_weight,
        *[resident(part) for part in held],
    )
    return stream, own, wires


def read_kernel(layer, sizes, count, held, late, *refs):
    local_heads, group_size, slots, head_size, stream_width, model_width = sizes
    terms = refs[:count]
    bias_ref, left_ref, right_ref, scale_ref = refs[count : count + 4]
    held_refs = refs[count + 4 : count + 4 + len(held)]
    rest = refs[count + 4 + len(held) :]
    own_ref, wire_ref, rows_ref, phi_ref, history_ref = rest[late:][:5]
    requests = own_ref.shape[0]
    block_feat = phi_ref.shape[1]
    if late:
        state_ref, late_ref, sem = rest[0], *rest[-2:]
        early = sum(held)
        copy = pltpu.make_async_copy(
            state_ref.at[layer, early:requests], late_ref.at[: requests - early], sem
        )
        copy.start()
    query_width = local_heads * group_size * head_size
    kv_width = local_heads * head_size
    own, others = terms[0], terms[1:]
    common = query_width + LANES
    total = add_terms([ref.at[:, :common] for ref in terms])
    extra = total[:, query_width:]
    half = LANES // 2
    extra = extra[:, :half] + extra[:, half:]
    inverse = lax.rsqrt(extra[:, 0:1] / model_width + EPS)
    queries = total[:, :query_width] * inverse

    feat_size = model_width // stream_width
    share = requests // feat_size
    mine = lax.axis_index("feat")
    if others[0].shape[1] == own.shape[1]:
        pairs = add_terms([ref.at[:, common:] for ref in terms])
        pairs = own_rows(pairs, share, mine)
    else:
        packed = add_terms([ref.at[:, common:] for ref in others])
        pairs = own_rows(own[:, common:], share, mine) + jnp.concatenate(
            [packed[at : at + share] for at in range(0, requests, share)], axis=1
        )
    pairs = jnp.concatenate([pairs] * feat_size, axis=0) * inverse
    block = lax.broadcasted_iota(jnp.int32, (requests, 1), 0) // share
    pairs = jnp.where(block == mine, pairs, 0.0)

    span = local_heads * slots
    for head in range(local_heads):
        for slot in range(slots):
            if slot < group_size:
                start = (head * group_size + slot) * head_size
                part = queries[:, start : start + head_size]
            else:
                part = jnp.zeros((requests, head_size), F32)
            rows_ref[pl.ds(head * slots + slot, requests, stride=span), :] = part
    vectors = jnp.concatenate(split(rows_ref[...]), axis=1)

    step = 2 * LANES
    for start in range(0, block_feat, step):
        stop = min(start + step, block_feat)
        left = jnp.dot(vectors, left_ref[:, start:stop], preferred_element_type=F32)
        right = jnp.dot(vectors, right_ref[:, start:stop], preferred_element_type=F32)
        phi_ref[:, start:stop] = (left * right * scale_ref[:, start:stop]).astype(BF16)

    def one_request(request, states):
        rows = phi_ref[request * span : (request + 1) * span, :]
        state = jnp.concatenate(states, axis=1) if local_heads > 1 else states[0]
        out = jnp.dot(rows, state, preferred_element_type=F32)
        for head in range(local_heads):
            at = head * slots
            history_ref[request * span + at : request * span + at + slots, :] = out[
                at : at + slots, head * head_size : (head + 1) * head_size
            ]

    request = 0
    for held_ref, many in zip(held_refs, held):
        for at in range(many):
            one_request(request, [held_ref[at, head] for head in range(local_heads)])
            request += 1
    if late:
        copy.wait()
        for at in range(requests - early):
            one_request(early + at, [late_ref[at, head] for head in range(local_heads)])

    for head in range(local_heads):
        logit = extra[:, head + 1 : head + 2] * inverse
        logit = logit + bias_ref[layer : layer + 1, head : head + 1]
        softplus = jnp.maximum(logit, 0.0) + jnp.log(1.0 + jnp.exp(-jnp.abs(logit)))
        decay = jnp.exp(-softplus)
        start = head * head_size
        key = pairs[:, start : start + head_size]
        value = pairs[:, start + kv_width : start + kv_width + head_size]
        for slot in range(group_size):
            start = (head * group_size + slot) * head_size
            query = queries[:, start : start + head_size]
            product = jnp.sum(query * key, axis=1, keepdims=True)
            cross = product * product / head_size
            part = decay * history_ref[pl.ds(head * slots + slot, requests, stride=span), :]
            part = part + cross * value
            own_ref[:, start : start + head_size] = part
            wire_ref[:, start : start + head_size] = part.astype(wire_ref.dtype)


def read(layer, sizes, wire, terms, gate_bias, picks, held, retained):
    local_heads, group_size, slots, head_size, _, _ = sizes
    requests = terms[0].shape[0]
    block_feat = picks[0].shape[1]
    width = local_heads * group_size * head_size
    counts = tuple(array.shape[0] for array in held)
    missing = requests - sum(counts)
    late = int(missing > 0)
    rows = requests * local_heads * slots
    return pl.pallas_call(
        functools.partial(read_kernel, layer, sizes, len(terms), counts, late),
        out_shape=[
            jax.ShapeDtypeStruct((requests, width), F32),
            jax.ShapeDtypeStruct((requests, width), wire),
        ],
        in_specs=[VMEM_SPEC] * (len(terms) + 4 + len(held)) + [HBM_SPEC] * late,
        out_specs=[VMEM_SPEC] * 2,
        scratch_shapes=[
            pltpu.VMEM((rows, head_size), F32),
            pltpu.VMEM((rows, block_feat), BF16),
            pltpu.VMEM((rows, head_size), F32),
        ]
        + [pltpu.VMEM((missing,) + retained.shape[2:], BF16), pltpu.SemaphoreType.DMA] * late,
        compiler_params=params(6 + 6 * late),
        name="read",
    )(
        *terms,
        gate_bias,
        *[resident(array) for array in (*picks, *held)],
        *[off_chip(retained)] * late,
    )


def mix_kernel(layer, count, held, *refs):
    terms = refs[:count]
    gain_ref, weight_ref = refs[count : count + 2]
    wire_ref, mixed_ref = refs[count + 2 + held :]
    head_size = gain_ref.shape[1]
    readout = add_terms(terms)
    gain = gain_ref[layer : layer + 1, :]
    for start in range(0, readout.shape[1], head_size):
        part = readout[:, start : start + head_size]
        mean = jnp.mean(part * part, axis=1, keepdims=True)
        mixed_ref[:, start : start + head_size] = part * lax.rsqrt(mean + EPS) * gain
    wire_ref[...] = split_dot(mixed_ref[...], weight_ref[layer]).astype(wire_ref.dtype)


def mix(layer, wire, terms, read_gain, weight, held):
    requests, rows = terms[0].shape
    return pl.pallas_call(
        functools.partial(mix_kernel, layer, len(terms), len(held)),
        out_shape=jax.ShapeDtypeStruct((requests, weight.shape[2]), wire),
        in_specs=[VMEM_SPEC] * (len(terms) + 2) + [ANY_SPEC] * len(held),
        out_specs=VMEM_SPEC,
        scratch_shapes=[pltpu.VMEM((requests, rows), F32)],
        compiler_params=params(8),
        name="mix",
    )(*terms, read_gain, resident(weight), *[resident(part) for part in held])


def finish_kernel(count, *refs):
    stream = refs[0][...].astype(F32) + add_terms(refs[1:count])
    refs[count][...] = stream.astype(BF16)


def finish(terms):
    return pl.pallas_call(
        functools.partial(finish_kernel, len(terms)),
        out_shape=jax.ShapeDtypeStruct(terms[0].shape, BF16),
        in_specs=[VMEM_SPEC] * len(terms),
        out_specs=VMEM_SPEC,
        compiler_params=params(2),
        name="finish",
    )(*terms)


def body(
    feat_size,
    head_ranks,
    token_ids,
    embedding,
    retained,
    query_weight,
    key_weight,
    value_weight,
    gate_weight,
    gate_bias,
    norm_gain,
    read_gain,
    out_weight,
):
    layer_count, requests, local_heads, block_feat, head_size = retained.shape
    group_size = query_weight.shape[2] // (local_heads * head_size)
    slots = -(-group_size // SUBLANES) * SUBLANES
    stream_width = norm_gain.shape[1]
    model_width = stream_width * feat_size
    sizes = (local_heads, group_size, slots, head_size, stream_width, model_width)
    feat_wire = wire_type(feat_size)
    head_wire = wire_type(head_ranks)
    weights = (query_weight, key_weight, value_weight)
    gate_rows = gate_weight.transpose(0, 2, 1)

    def fetch_state(layer, stage):
        shares = LATER_LAYER if layer else FIRST_LAYER
        start = requests * sum(shares[:stage]) // sum(shares)
        stop = requests * sum(shares[: stage + 1]) // sum(shares)
        if layer >= layer_count or start == stop:
            return []
        return list(fetch([retained], ((0, (layer, slice(start, stop))),)))

    picked, picks = pick_rows(token_ids, embedding, head_size, block_feat)
    stream_terms = exchange(picked, [picked], "head", head_ranks)
    carried, held = [], []
    for layer in range(layer_count):
        held = held + fetch_state(layer, 1)
        stream, own, wires = project(
            layer, carried, feat_size, stream_terms, norm_gain, weights, gate_rows, held
        )
        terms = exchange(own, wires, "feat", feat_size)
        held = held + fetch_state(layer, 2)
        own, wire = read(layer, sizes, feat_wire, terms, gate_bias, picks, held, retained)
        terms = exchange(own, [wire], "feat", feat_size)
        held = fetch_state(layer + 1, 0)
        wire = mix(layer, head_wire, terms, read_gain, out_weight, held)
        stream_terms = exchange(wire, [wire], "head", head_ranks)
        carried = [stream]
    return finish(carried + stream_terms)


def solution(mesh):
    return jax.shard_map(
        functools.partial(body, mesh.shape["feat"], mesh.shape["head"]),
        mesh=mesh,
        in_specs=(
            P("groups"),
            P("head", "feat"),
            P(None, "groups", "head", "feat", None),
            P(None, "feat", "head"),
            P(None, "feat", "head"),
            P(None, "feat", "head"),
            P(None, "feat", "head"),
            P(None, "head"),
            P(None, "feat"),
            P(),
            P(None, "head", "feat"),
        ),
        out_specs=P("groups", "feat"),
        check_vma=False,
    )
```

```python
import functools
import math

import jax
import jax.numpy as jnp
from jax import lax
from jax.experimental import pallas as pl
from jax.experimental.pallas import tpu as pltpu
from jax.sharding import PartitionSpec as P

EPS = 1e-6
LANES = 128
SUBLANES = 8
ROWS = 16
FIRST_LAYER = (0, 3, 9, 4)
LATER_LAYER = (5, 4, 7, 0)
MIB = 2**20
F32 = jnp.float32
BF16 = jnp.bfloat16

VMEM_SPEC = pl.BlockSpec(memory_space=pltpu.VMEM)
ANY_SPEC = pl.BlockSpec(memory_space=pl.ANY)
HBM_SPEC = pl.BlockSpec(memory_space=pltpu.HBM)
SMEM_SPEC = pl.BlockSpec(memory_space=pltpu.SMEM)


def params(mib):
    return pltpu.CompilerParams(vmem_limit_bytes=mib * MIB)


def resident(array):
    return pltpu.with_memory_space_constraint(array, pltpu.VMEM)


def off_chip(array):
    return pltpu.with_memory_space_constraint(array, pltpu.HBM)


def wire_type(size):
    return BF16 if size <= 4 else F32


def steps_of(size, axis):
    if size > 4:
        return ()
    order = (2, 3, 1) if axis == "feat" else (3, 2, 1)
    return tuple(step for step in order if step < size)


def exchange(own, wires, axis, size):
    steps = steps_of(size, axis)
    if not steps:
        (wire,) = wires
        return [own.astype(F32) - wire.astype(F32), lax.psum(wire.astype(F32), axis)]
    if len(wires) == 1:
        wires = wires * len(steps)
    return [own] + [
        lax.ppermute(wire, axis, [(rank, rank ^ step) for rank in range(size)])
        for wire, step in zip(wires, steps)
    ]


def own_rows(array, share, mine):
    rows = array[:share]
    for block in range(1, array.shape[0] // share):
        rows = jnp.where(mine == block, array[block * share : (block + 1) * share], rows)
    return rows


def split(wide):
    high = wide.astype(BF16)
    return high, (wide - high.astype(F32)).astype(BF16)


def split_dot(wide, weight):
    rows = wide.shape[0]
    out = jnp.dot(jnp.concatenate(split(wide), axis=0), weight, preferred_element_type=F32)
    return out[:rows] + out[rows:]


def add_terms(refs):
    terms = [ref[...].astype(F32) for ref in refs]
    while len(terms) > 1:
        terms = [sum(terms[at : at + 2]) for at in range(0, len(terms), 2)]
    return terms[0]


def make_selectors(left_ref, right_ref, scale_ref):
    depth, block_feat = left_ref.shape
    size = depth // 2

    def first_of(row):
        return row * size - row * (row - 1) // 2

    column = lax.broadcasted_iota(jnp.int32, (1, block_feat), 1)
    feature = lax.axis_index("feat") * block_feat + column
    reach = 2 * size + 1
    root = jnp.sqrt((reach * reach - 8 * feature).astype(F32))
    left = ((reach - root) * 0.5).astype(jnp.int32)
    left = jnp.where(first_of(left) > feature, left - 1, left)
    left = jnp.where(first_of(left + 1) <= feature, left + 1, left)
    right = feature - first_of(left) + left
    at = lax.broadcasted_iota(jnp.int32, left_ref.shape, 0)
    at = jnp.where(at >= size, at - size, at)
    left_ref[...] = jnp.where(at == left, 1.0, 0.0).astype(BF16)
    right_ref[...] = jnp.where(at == right, 1.0, 0.0).astype(BF16)
    scale_ref[...] = jnp.where(left == right, 1.0, math.sqrt(2.0)).astype(F32)


def pick_kernel(ids_ref, table_ref, out_ref, left_ref, right_ref, scale_ref, groups_ref, sems):
    requests = out_ref.shape[0]
    table_rows = table_ref.shape[0]
    row_start = lax.axis_index("head") * table_rows
    row_at = lax.broadcasted_iota(jnp.int32, (requests, requests * ROWS), 0)
    column_at = lax.broadcasted_iota(jnp.int32, (requests, requests * ROWS), 1)
    chosen = jnp.zeros((requests, requests * ROWS), F32)
    groups_ref[...] = jnp.zeros_like(groups_ref)
    copies = []
    for request in range(requests):
        local_id = ids_ref[request] - row_start
        inside = (local_id >= 0) & (local_id < table_rows)
        row = jnp.clip(local_id, 0, table_rows - 1)
        first = pl.multiple_of((row // ROWS) * ROWS, ROWS)
        copy = pltpu.make_async_copy(
            table_ref.at[pl.ds(first, ROWS), :],
            groups_ref.at[pl.ds(request * ROWS, ROWS), :],
            sems.at[request],
        )
        pl.when(inside)(copy.start)
        copies.append((inside, copy))
        place = jnp.where(inside, request * ROWS + row - first, -1)
        chosen = jnp.where((row_at == request) & (column_at == place), 1.0, chosen)
    make_selectors(left_ref, right_ref, scale_ref)
    for inside, copy in copies:
        pl.when(inside)(copy.wait)
    out_ref[...] = jnp.dot(
        chosen.astype(BF16), groups_ref[...], preferred_element_type=F32
    ).astype(BF16)


def pick_rows(token_ids, embedding, head_size, block_feat):
    table_rows, width = embedding.shape
    requests = token_ids.shape[0]
    picks = [
        pltpu.VMEM((2 * head_size, block_feat), BF16),
        pltpu.VMEM((2 * head_size, block_feat), BF16),
        pltpu.VMEM((1, block_feat), F32),
    ]
    if table_rows % ROWS:
        picks = pl.pallas_call(
            make_selectors,
            out_shape=picks,
            out_specs=[VMEM_SPEC] * 3,
            compiler_params=params(8),
            name="selectors",
        )()
        local_ids = token_ids - lax.axis_index("head") * table_rows
        inside = (local_ids >= 0) & (local_ids < table_rows)
        picked = jnp.take(embedding, jnp.clip(local_ids, 0, table_rows - 1), axis=0)
        return jnp.where(inside[:, None], picked, jnp.zeros_like(picked)), picks
    picked, *picks = pl.pallas_call(
        pick_kernel,
        out_shape=[jax.ShapeDtypeStruct((requests, width), BF16)] + picks,
        in_specs=[SMEM_SPEC, HBM_SPEC],
        out_specs=[VMEM_SPEC] * 4,
        scratch_shapes=[
            pltpu.VMEM((requests * ROWS, width), BF16),
            pltpu.SemaphoreType.DMA((requests,)),
        ],
        compiler_params=params(8),
        name="pick_rows",
    )(off_chip(token_ids), off_chip(embedding))
    return picked, picks


def fetch_kernel(plan, count, *refs):
    sources, outs, sems = refs[:count], refs[count:-1], refs[-1]
    copies = []
    for at, (source, index) in enumerate(plan):
        copy = pltpu.make_async_copy(sources[source].at[index], outs[at], sems.at[at])
        copy.start()
        copies.append(copy)
    for copy in copies:
        copy.wait()


def fetch(sources, plan):
    shapes = []
    for source, index in plan:
        array = sources[source]
        index = index if isinstance(index, tuple) else (index,)
        shape = []
        for at, extent in enumerate(array.shape):
            if at >= len(index):
                shape.append(extent)
            elif isinstance(index[at], slice):
                shape.append(index[at].stop - index[at].start)
        shapes.append(pltpu.VMEM(tuple(shape), array.dtype))
    return pl.pallas_call(
        functools.partial(fetch_kernel, plan, len(sources)),
        out_shape=shapes,
        in_specs=[HBM_SPEC] * len(sources),
        out_specs=[VMEM_SPEC] * len(plan),
        scratch_shapes=[pltpu.SemaphoreType.DMA((len(plan),))],
        compiler_params=params(2),
        name="fetch",
    )(*[off_chip(source) for source in sources])


def project_kernel(layer, count, carried, held, steps, *refs):
    terms = refs[carried:count]
    gain_ref, query_ref, key_ref, value_ref, gate_ref = refs[count : count + 5]
    stream_ref, own_ref, *wire_refs = refs[count + 5 + held :]
    stream = add_terms(terms)
    if carried:
        stream = refs[0][...].astype(F32) + stream
    stream = stream.astype(BF16)
    stream_ref[...] = stream
    wide = stream.astype(F32)
    sum_sq = jnp.sum(wide * wide, axis=1, keepdims=True)
    scaled = wide * gain_ref[layer : layer + 1, :]
    parts = [
        split_dot(scaled, weight_ref[layer]) for weight_ref in (query_ref, key_ref, value_ref)
    ]
    requests = stream.shape[0]
    lane = lax.broadcasted_iota(jnp.int32, (requests, LANES), 1)
    half = LANES // 2
    place = jnp.where(lane >= half, lane - half, lane)
    extra = jnp.where(place == 0, sum_sq, 0.0)
    for head in range(gate_ref.shape[1]):
        column = gate_ref[layer, head : head + 1, :].astype(F32)
        gate = jnp.sum(scaled * column, axis=1, keepdims=True)
        extra = jnp.where(place == head + 1, gate, extra)
    rounded = extra.astype(BF16).astype(F32)
    sent = jnp.where(lane < half, rounded, extra - rounded)
    kept = jnp.where(lane < half, extra, 0.0)
    start = 0
    for part, other in zip((parts[0], kept, *parts[1:]), (parts[0], sent, *parts[1:])):
        stop = start + part.shape[1]
        own_ref[:, start:stop] = part
        for wire_ref in wire_refs:
            if stop <= wire_ref.shape[1]:
                wire_ref[:, start:stop] = other.astype(wire_ref.dtype)
        start = stop
    for step, wire_ref in zip(steps, wire_refs):
        share = requests // (len(steps) + 1)
        partner = lax.axis_index("feat") ^ step
        packed = [
            own_rows(part[:, at : at + LANES], share, partner)
            for part in parts[1:]
            for at in range(0, part.shape[1], LANES)
        ]
        wire_ref[:, -LANES:] = jnp.concatenate(packed, axis=0).astype(wire_ref.dtype)


def packs(requests, weights, size):
    blocks = sum(weight.shape[2] for weight in weights[1:]) // LANES
    return len(steps_of(size, "feat")) > 0 and blocks == size and requests % size == 0


def project(layer, carried, size, terms, norm_gain, weights, gate_weight, held):
    terms = carried + terms
    requests, width = terms[0].shape
    query_width = weights[0].shape[2]
    total = sum(weight.shape[2] for weight in weights) + LANES
    if packs(requests, weights, size):
        steps, sent = steps_of(size, "feat"), query_width + 2 * LANES
    else:
        steps, sent = (), total
    wires = [jax.ShapeDtypeStruct((requests, sent), wire_type(size))] * max(len(steps), 1)
    stream, own, *wires = pl.pallas_call(
        functools.partial(project_kernel, layer, len(terms), len(carried), len(held), steps),
        out_shape=[
            jax.ShapeDtypeStruct((requests, width), BF16),
            jax.ShapeDtypeStruct((requests, total), F32),
        ]
        + wires,
        in_specs=[VMEM_SPEC] * (len(terms) + 5) + [ANY_SPEC] * len(held),
        out_specs=[VMEM_SPEC] * (2 + len(wires)),
        compiler_params=params(8),
        name="project",
    )(
        *terms,
        norm_gain,
        *[resident(weight) for weight in weights],
        gate_weight,
        *[resident(part) for part in held],
    )
    return stream, own, wires


def read_kernel(layer, sizes, count, held, late, *refs):
    local_heads, group_size, slots, head_size, stream_width, model_width = sizes
    terms = refs[:count]
    bias_ref, left_ref, right_ref, scale_ref = refs[count : count + 4]
    held_refs = refs[count + 4 : count + 4 + len(held)]
    rest = refs[count + 4 + len(held) :]
    own_ref, wire_ref, rows_ref, phi_ref, history_ref = rest[late:][:5]
    requests = own_ref.shape[0]
    block_feat = phi_ref.shape[1]
    if late:
        state_ref, late_ref, sem = rest[0], *rest[-2:]
        early = sum(held)
        copy = pltpu.make_async_copy(
            state_ref.at[layer, early:requests], late_ref.at[: requests - early], sem
        )
        copy.start()
    query_width = local_heads * group_size * head_size
    kv_width = local_heads * head_size
    own, others = terms[0], terms[1:]
    common = query_width + LANES
    total = add_terms([ref.at[:, :common] for ref in terms])
    extra = total[:, query_width:]
    half = LANES // 2
    extra = extra[:, :half] + extra[:, half:]
    inverse = lax.rsqrt(extra[:, 0:1] / model_width + EPS)
    queries = total[:, :query_width] * inverse

    feat_size = model_width // stream_width
    share = requests // feat_size
    mine = lax.axis_index("feat")
    if others[0].shape[1] == own.shape[1]:
        pairs = add_terms([ref.at[:, common:] for ref in terms])
        pairs = own_rows(pairs, share, mine)
    else:
        packed = add_terms([ref.at[:, common:] for ref in others])
        pairs = own_rows(own[:, common:], share, mine) + jnp.concatenate(
            [packed[at : at + share] for at in range(0, requests, share)], axis=1
        )
    pairs = jnp.concatenate([pairs] * feat_size, axis=0) * inverse
    block = lax.broadcasted_iota(jnp.int32, (requests, 1), 0) // share
    pairs = jnp.where(block == mine, pairs, 0.0)

    span = local_heads * slots
    for head in range(local_heads):
        for slot in range(slots):
            if slot < group_size:
                start = (head * group_size + slot) * head_size
                part = queries[:, start : start + head_size]
            else:
                part = jnp.zeros((requests, head_size), F32)
            rows_ref[pl.ds(head * slots + slot, requests, stride=span), :] = part
    vectors = jnp.concatenate(split(rows_ref[...]), axis=1)

    step = 2 * LANES
    for start in range(0, block_feat, step):
        stop = min(start + step, block_feat)
        left = jnp.dot(vectors, left_ref[:, start:stop], preferred_element_type=F32)
        right = jnp.dot(vectors, right_ref[:, start:stop], preferred_element_type=F32)
        phi_ref[:, start:stop] = (left * right * scale_ref[:, start:stop]).astype(BF16)

    def one_request(request, states):
        rows = phi_ref[request * span : (request + 1) * span, :]
        state = jnp.concatenate(states, axis=1) if local_heads > 1 else states[0]
        out = jnp.dot(rows, state, preferred_element_type=F32)
        for head in range(local_heads):
            at = head * slots
            history_ref[request * span + at : request * span + at + slots, :] = out[
                at : at + slots, head * head_size : (head + 1) * head_size
            ]

    request = 0
    for held_ref, many in zip(held_refs, held):
        for at in range(many):
            one_request(request, [held_ref[at, head] for head in range(local_heads)])
            request += 1
    if late:
        copy.wait()
        for at in range(requests - early):
            one_request(early + at, [late_ref[at, head] for head in range(local_heads)])

    for head in range(local_heads):
        logit = extra[:, head + 1 : head + 2] * inverse
        logit = logit + bias_ref[layer : layer + 1, head : head + 1]
        softplus = jnp.maximum(logit, 0.0) + jnp.log(1.0 + jnp.exp(-jnp.abs(logit)))
        decay = jnp.exp(-softplus)
        start = head * head_size
        key = pairs[:, start : start + head_size]
        value = pairs[:, start + kv_width : start + kv_width + head_size]
        for slot in range(group_size):
            start = (head * group_size + slot) * head_size
            query = queries[:, start : start + head_size]
            product = jnp.sum(query * key, axis=1, keepdims=True)
            cross = product * product / head_size
            part = decay * history_ref[pl.ds(head * slots + slot, requests, stride=span), :]
            part = part + cross * value
            own_ref[:, start : start + head_size] = part
            wire_ref[:, start : start + head_size] = part.astype(wire_ref.dtype)


def read(layer, sizes, wire, terms, gate_bias, picks, held, retained):
    local_heads, group_size, slots, head_size, _, _ = sizes
    requests = terms[0].shape[0]
    block_feat = picks[0].shape[1]
    width = local_heads * group_size * head_size
    counts = tuple(array.shape[0] for array in held)
    missing = requests - sum(counts)
    late = int(missing > 0)
    rows = requests * local_heads * slots
    return pl.pallas_call(
        functools.partial(read_kernel, layer, sizes, len(terms), counts, late),
        out_shape=[
            jax.ShapeDtypeStruct((requests, width), F32),
            jax.ShapeDtypeStruct((requests, width), wire),
        ],
        in_specs=[VMEM_SPEC] * (len(terms) + 4 + len(held)) + [HBM_SPEC] * late,
        out_specs=[VMEM_SPEC] * 2,
        scratch_shapes=[
            pltpu.VMEM((rows, head_size), F32),
            pltpu.VMEM((rows, block_feat), BF16),
            pltpu.VMEM((rows, head_size), F32),
        ]
        + [pltpu.VMEM((missing,) + retained.shape[2:], BF16), pltpu.SemaphoreType.DMA] * late,
        compiler_params=params(6 + 6 * late),
        name="read",
    )(
        *terms,
        gate_bias,
        *[resident(array) for array in (*picks, *held)],
        *[off_chip(retained)] * late,
    )


def mix_kernel(layer, count, held, *refs):
    terms = refs[:count]
    gain_ref, weight_ref = refs[count : count + 2]
    wire_ref, mixed_ref = refs[count + 2 + held :]
    head_size = gain_ref.shape[1]
    readout = add_terms(terms)
    gain = gain_ref[layer : layer + 1, :]
    for start in range(0, readout.shape[1], head_size):
        part = readout[:, start : start + head_size]
        mean = jnp.mean(part * part, axis=1, keepdims=True)
        mixed_ref[:, start : start + head_size] = part * lax.rsqrt(mean + EPS) * gain
    wire_ref[...] = split_dot(mixed_ref[...], weight_ref[layer]).astype(wire_ref.dtype)


def mix(layer, wire, terms, read_gain, weight, held):
    requests, rows = terms[0].shape
    return pl.pallas_call(
        functools.partial(mix_kernel, layer, len(terms), len(held)),
        out_shape=jax.ShapeDtypeStruct((requests, weight.shape[2]), wire),
        in_specs=[VMEM_SPEC] * (len(terms) + 2) + [ANY_SPEC] * len(held),
        out_specs=VMEM_SPEC,
        scratch_shapes=[pltpu.VMEM((requests, rows), F32)],
        compiler_params=params(8),
        name="mix",
    )(*terms, read_gain, resident(weight), *[resident(part) for part in held])


def finish_kernel(count, *refs):
    stream = refs[0][...].astype(F32) + add_terms(refs[1:count])
    refs[count][...] = stream.astype(BF16)


def finish(terms):
    return pl.pallas_call(
        functools.partial(finish_kernel, len(terms)),
        out_shape=jax.ShapeDtypeStruct(terms[0].shape, BF16),
        in_specs=[VMEM_SPEC] * len(terms),
        out_specs=VMEM_SPEC,
        compiler_params=params(2),
        name="finish",
    )(*terms)


def body(
    feat_size,
    head_ranks,
    token_ids,
    embedding,
    retained,
    query_weight,
    key_weight,
    value_weight,
    gate_weight,
    gate_bias,
    norm_gain,
    read_gain,
    out_weight,
):
    layer_count, requests, local_heads, block_feat, head_size = retained.shape
    group_size = query_weight.shape[2] // (local_heads * head_size)
    slots = -(-group_size // SUBLANES) * SUBLANES
    stream_width = norm_gain.shape[1]
    model_width = stream_width * feat_size
    sizes = (local_heads, group_size, slots, head_size, stream_width, model_width)
    feat_wire = wire_type(feat_size)
    head_wire = wire_type(head_ranks)
    weights = (query_weight, key_weight, value_weight)
    gate_rows = gate_weight.transpose(0, 2, 1)

    def fetch_state(layer, stage):
        shares = LATER_LAYER if layer else FIRST_LAYER
        start = requests * sum(shares[:stage]) // sum(shares)
        stop = requests * sum(shares[: stage + 1]) // sum(shares)
        if layer >= layer_count or start == stop:
            return []
        return list(fetch([retained], ((0, (layer, slice(start, stop))),)))

    picked, picks = pick_rows(token_ids, embedding, head_size, block_feat)
    stream_terms = exchange(picked, [picked], "head", head_ranks)
    carried, held = [], []
    for layer in range(layer_count):
        held = held + fetch_state(layer, 1)
        stream, own, wires = project(
            layer, carried, feat_size, stream_terms, norm_gain, weights, gate_rows, held
        )
        terms = exchange(own, wires, "feat", feat_size)
        held = held + fetch_state(layer, 2)
        own, wire = read(layer, sizes, feat_wire, terms, gate_bias, picks, held, retained)
        terms = exchange(own, [wire], "feat", feat_size)
        held = fetch_state(layer + 1, 0)
        wire = mix(layer, head_wire, terms, read_gain, out_weight, held)
        stream_terms = exchange(wire, [wire], "head", head_ranks)
        carried = [stream]
    return finish(carried + stream_terms)


def solution(mesh):
    return jax.shard_map(
        functools.partial(body, mesh.shape["feat"], mesh.shape["head"]),
        mesh=mesh,
        in_specs=(
            P("groups"),
            P("head", "feat"),
            P(None, "groups", "head", "feat", None),
            P(None, "feat", "head"),
            P(None, "feat", "head"),
            P(None, "feat", "head"),
            P(None, "feat", "head"),
            P(None, "head"),
            P(None, "feat"),
            P(),
            P(None, "head", "feat"),
        ),
        out_specs=P("groups", "feat"),
        check_vma=False,
    )
```

```python
import functools
import math

import jax
import jax.numpy as jnp
from jax import lax
from jax.experimental import pallas as pl
from jax.experimental.pallas import tpu as pltpu
from jax.sharding import PartitionSpec as P

EPS = 1e-6
LANES = 128
SUBLANES = 8
ROWS = 16
FIRST_LAYER = (0, 4, 8, 4)
LATER_LAYER = (5, 4, 7, 0)
MIB = 2**20
F32 = jnp.float32
BF16 = jnp.bfloat16

VMEM_SPEC = pl.BlockSpec(memory_space=pltpu.VMEM)
ANY_SPEC = pl.BlockSpec(memory_space=pl.ANY)
HBM_SPEC = pl.BlockSpec(memory_space=pltpu.HBM)
SMEM_SPEC = pl.BlockSpec(memory_space=pltpu.SMEM)


def params(mib):
    return pltpu.CompilerParams(vmem_limit_bytes=mib * MIB)


def resident(array):
    return pltpu.with_memory_space_constraint(array, pltpu.VMEM)


def off_chip(array):
    return pltpu.with_memory_space_constraint(array, pltpu.HBM)


def wire_type(size):
    return BF16 if size <= 4 else F32


def steps_of(size, axis):
    if size > 4:
        return ()
    order = (2, 3, 1) if axis == "feat" else (3, 2, 1)
    return tuple(step for step in order if step < size)


def exchange(own, wires, axis, size):
    steps = steps_of(size, axis)
    if not steps:
        (wire,) = wires
        return [own.astype(F32) - wire.astype(F32), lax.psum(wire.astype(F32), axis)]
    if len(wires) == 1:
        wires = wires * len(steps)
    return [own] + [
        lax.ppermute(wire, axis, [(rank, rank ^ step) for rank in range(size)])
        for wire, step in zip(wires, steps)
    ]


def own_rows(array, share, mine):
    rows = array[:share]
    for block in range(1, array.shape[0] // share):
        rows = jnp.where(mine == block, array[block * share : (block + 1) * share], rows)
    return rows


def split(wide):
    high = wide.astype(BF16)
    return high, (wide - high.astype(F32)).astype(BF16)


def split_dot(wide, weight):
    rows, depth = wide.shape
    empty = jnp.zeros((max(LANES - 2 * rows, 0), depth), BF16)
    parts = jnp.concatenate((*split(wide), empty), axis=0)
    out = jnp.dot(parts, weight, preferred_element_type=F32)
    return out[:rows] + out[rows : 2 * rows]


def add_terms(refs):
    terms = [ref[...].astype(F32) for ref in refs]
    while len(terms) > 1:
        terms = [sum(terms[at : at + 2]) for at in range(0, len(terms), 2)]
    return terms[0]


def make_selectors(left_ref, right_ref, scale_ref):
    depth, block_feat = left_ref.shape
    size = depth // 2

    def first_of(row):
        return row * size - row * (row - 1) // 2

    column = lax.broadcasted_iota(jnp.int32, (1, block_feat), 1)
    feature = lax.axis_index("feat") * block_feat + column
    reach = 2 * size + 1
    root = jnp.sqrt((reach * reach - 8 * feature).astype(F32))
    left = ((reach - root) * 0.5).astype(jnp.int32)
    left = jnp.where(first_of(left) > feature, left - 1, left)
    left = jnp.where(first_of(left + 1) <= feature, left + 1, left)
    right = feature - first_of(left) + left
    at = lax.broadcasted_iota(jnp.int32, left_ref.shape, 0)
    at = jnp.where(at >= size, at - size, at)
    left_ref[...] = jnp.where(at == left, 1.0, 0.0).astype(BF16)
    right_ref[...] = jnp.where(at == right, 1.0, 0.0).astype(BF16)
    scale_ref[...] = jnp.where(left == right, 1.0, math.sqrt(2.0)).astype(F32)


def pick_kernel(ids_ref, table_ref, out_ref, left_ref, right_ref, scale_ref, groups_ref, sems):
    requests = out_ref.shape[0]
    table_rows = table_ref.shape[0]
    row_start = lax.axis_index("head") * table_rows
    row_at = lax.broadcasted_iota(jnp.int32, (requests, requests * ROWS), 0)
    column_at = lax.broadcasted_iota(jnp.int32, (requests, requests * ROWS), 1)
    chosen = jnp.zeros((requests, requests * ROWS), F32)
    groups_ref[...] = jnp.zeros_like(groups_ref)
    copies = []
    for request in range(requests):
        local_id = ids_ref[request] - row_start
        inside = (local_id >= 0) & (local_id < table_rows)
        row = jnp.clip(local_id, 0, table_rows - 1)
        first = pl.multiple_of((row // ROWS) * ROWS, ROWS)
        copy = pltpu.make_async_copy(
            table_ref.at[pl.ds(first, ROWS), :],
            groups_ref.at[pl.ds(request * ROWS, ROWS), :],
            sems.at[request],
        )
        pl.when(inside)(copy.start)
        copies.append((inside, copy))
        place = jnp.where(inside, request * ROWS + row - first, -1)
        chosen = jnp.where((row_at == request) & (column_at == place), 1.0, chosen)
    make_selectors(left_ref, right_ref, scale_ref)
    for inside, copy in copies:
        pl.when(inside)(copy.wait)
    out_ref[...] = jnp.dot(
        chosen.astype(BF16), groups_ref[...], preferred_element_type=F32
    ).astype(BF16)


def pick_rows(token_ids, embedding, head_size, block_feat):
    table_rows, width = embedding.shape
    requests = token_ids.shape[0]
    picks = [
        pltpu.VMEM((2 * head_size, block_feat), BF16),
        pltpu.VMEM((2 * head_size, block_feat), BF16),
        pltpu.VMEM((1, block_feat), F32),
    ]
    if table_rows % ROWS:
        picks = pl.pallas_call(
            make_selectors,
            out_shape=picks,
            out_specs=[VMEM_SPEC] * 3,
            compiler_params=params(8),
            name="selectors",
        )()
        local_ids = token_ids - lax.axis_index("head") * table_rows
        inside = (local_ids >= 0) & (local_ids < table_rows)
        picked = jnp.take(embedding, jnp.clip(local_ids, 0, table_rows - 1), axis=0)
        return jnp.where(inside[:, None], picked, jnp.zeros_like(picked)), picks
    picked, *picks = pl.pallas_call(
        pick_kernel,
        out_shape=[jax.ShapeDtypeStruct((requests, width), BF16)] + picks,
        in_specs=[SMEM_SPEC, HBM_SPEC],
        out_specs=[VMEM_SPEC] * 4,
        scratch_shapes=[
            pltpu.VMEM((requests * ROWS, width), BF16),
            pltpu.SemaphoreType.DMA((requests,)),
        ],
        compiler_params=params(8),
        name="pick_rows",
    )(off_chip(token_ids), off_chip(embedding))
    return picked, picks


def fetch_kernel(plan, count, *refs):
    sources, outs, sems = refs[:count], refs[count:-1], refs[-1]
    copies = []
    for at, (source, index) in enumerate(plan):
        copy = pltpu.make_async_copy(sources[source].at[index], outs[at], sems.at[at])
        copy.start()
        copies.append(copy)
    for copy in copies:
        copy.wait()


def fetch(sources, plan):
    shapes = []
    for source, index in plan:
        array = sources[source]
        index = index if isinstance(index, tuple) else (index,)
        shape = []
        for at, extent in enumerate(array.shape):
            if at >= len(index):
                shape.append(extent)
            elif isinstance(index[at], slice):
                shape.append(index[at].stop - index[at].start)
        shapes.append(pltpu.VMEM(tuple(shape), array.dtype))
    return pl.pallas_call(
        functools.partial(fetch_kernel, plan, len(sources)),
        out_shape=shapes,
        in_specs=[HBM_SPEC] * len(sources),
        out_specs=[VMEM_SPEC] * len(plan),
        scratch_shapes=[pltpu.SemaphoreType.DMA((len(plan),))],
        compiler_params=params(2),
        name="fetch",
    )(*[off_chip(source) for source in sources])


def project_kernel(layer, count, carried, held, steps, *refs):
    terms = refs[carried:count]
    gain_ref, query_ref, key_ref, value_ref, gate_ref = refs[count : count + 5]
    stream_ref, own_ref, *wire_refs = refs[count + 5 + held :]
    stream = add_terms(terms)
    if carried:
        stream = refs[0][...].astype(F32) + stream
    stream = stream.astype(BF16)
    stream_ref[...] = stream
    wide = stream.astype(F32)
    sum_sq = jnp.sum(wide * wide, axis=1, keepdims=True)
    scaled = wide * gain_ref[layer : layer + 1, :]
    parts = [
        split_dot(scaled, weight_ref[layer]) for weight_ref in (query_ref, key_ref, value_ref)
    ]
    requests = stream.shape[0]
    lane = lax.broadcasted_iota(jnp.int32, (requests, LANES), 1)
    half = LANES // 2
    place = jnp.where(lane >= half, lane - half, lane)
    extra = jnp.where(place == 0, sum_sq, 0.0)
    for head in range(gate_ref.shape[1]):
        column = gate_ref[layer, head : head + 1, :].astype(F32)
        gate = jnp.sum(scaled * column, axis=1, keepdims=True)
        extra = jnp.where(place == head + 1, gate, extra)
    rounded = extra.astype(BF16).astype(F32)
    sent = jnp.where(lane < half, rounded, extra - rounded)
    kept = jnp.where(lane < half, extra, 0.0)
    start = 0
    for part, other in zip((parts[0], kept, *parts[1:]), (parts[0], sent, *parts[1:])):
        stop = start + part.shape[1]
        own_ref[:, start:stop] = part
        for wire_ref in wire_refs:
            if stop <= wire_ref.shape[1]:
                wire_ref[:, start:stop] = other.astype(wire_ref.dtype)
        start = stop
    for step, wire_ref in zip(steps, wire_refs):
        share = requests // (len(steps) + 1)
        partner = lax.axis_index("feat") ^ step
        packed = [
            own_rows(part[:, at : at + LANES], share, partner)
            for part in parts[1:]
            for at in range(0, part.shape[1], LANES)
        ]
        wire_ref[:, -LANES:] = jnp.concatenate(packed, axis=0).astype(wire_ref.dtype)


def packs(requests, weights, size):
    blocks = sum(weight.shape[2] for weight in weights[1:]) // LANES
    return len(steps_of(size, "feat")) > 0 and blocks == size and requests % size == 0


def project(layer, carried, size, terms, norm_gain, weights, gate_weight, held):
    terms = carried + terms
    requests, width = terms[0].shape
    query_width = weights[0].shape[2]
    total = sum(weight.shape[2] for weight in weights) + LANES
    if packs(requests, weights, size):
        steps, sent = steps_of(size, "feat"), query_width + 2 * LANES
    else:
        steps, sent = (), total
    wires = [jax.ShapeDtypeStruct((requests, sent), wire_type(size))] * max(len(steps), 1)
    stream, own, *wires = pl.pallas_call(
        functools.partial(project_kernel, layer, len(terms), len(carried), len(held), steps),
        out_shape=[
            jax.ShapeDtypeStruct((requests, width), BF16),
            jax.ShapeDtypeStruct((requests, total), F32),
        ]
        + wires,
        in_specs=[VMEM_SPEC] * (len(terms) + 5) + [ANY_SPEC] * len(held),
        out_specs=[VMEM_SPEC] * (2 + len(wires)),
        compiler_params=params(8),
        name="project",
    )(
        *terms,
        norm_gain,
        *[resident(weight) for weight in weights],
        gate_weight,
        *[resident(part) for part in held],
    )
    return stream, own, wires


def read_kernel(layer, sizes, count, held, late, *refs):
    local_heads, group_size, slots, head_size, stream_width, model_width = sizes
    terms = refs[:count]
    bias_ref, left_ref, right_ref, scale_ref = refs[count : count + 4]
    held_refs = refs[count + 4 : count + 4 + len(held)]
    rest = refs[count + 4 + len(held) :]
    own_ref, wire_ref, rows_ref, phi_ref, history_ref = rest[late:][:5]
    requests = own_ref.shape[0]
    block_feat = phi_ref.shape[1]
    if late:
        state_ref, late_ref, sem = rest[0], *rest[-2:]
        early = sum(held)
        copy = pltpu.make_async_copy(
            state_ref.at[layer, early:requests], late_ref.at[: requests - early], sem
        )
        copy.start()
    query_width = local_heads * group_size * head_size
    kv_width = local_heads * head_size
    own, others = terms[0], terms[1:]
    common = query_width + LANES
    total = add_terms([ref.at[:, :common] for ref in terms])
    extra = total[:, query_width:]
    half = LANES // 2
    extra = extra[:, :half] + extra[:, half:]
    inverse = lax.rsqrt(extra[:, 0:1] / model_width + EPS)
    queries = total[:, :query_width] * inverse

    feat_size = model_width // stream_width
    share = requests // feat_size
    mine = lax.axis_index("feat")
    if others[0].shape[1] == own.shape[1]:
        pairs = add_terms([ref.at[:, common:] for ref in terms])
        pairs = own_rows(pairs, share, mine)
    else:
        packed = add_terms([ref.at[:, common:] for ref in others])
        pairs = own_rows(own[:, common:], share, mine) + jnp.concatenate(
            [packed[at : at + share] for at in range(0, requests, share)], axis=1
        )
    pairs = jnp.concatenate([pairs] * feat_size, axis=0) * inverse
    block = lax.broadcasted_iota(jnp.int32, (requests, 1), 0) // share
    pairs = jnp.where(block == mine, pairs, 0.0)

    span = local_heads * slots
    for head in range(local_heads):
        for slot in range(slots):
            if slot < group_size:
                start = (head * group_size + slot) * head_size
                part = queries[:, start : start + head_size]
            else:
                part = jnp.zeros((requests, head_size), F32)
            rows_ref[pl.ds(head * slots + slot, requests, stride=span), :] = part
    vectors = jnp.concatenate(split(rows_ref[...]), axis=1)

    step = 2 * LANES
    for start in range(0, block_feat, step):
        stop = min(start + step, block_feat)
        left = jnp.dot(vectors, left_ref[:, start:stop], preferred_element_type=F32)
        right = jnp.dot(vectors, right_ref[:, start:stop], preferred_element_type=F32)
        phi_ref[:, start:stop] = (left * right * scale_ref[:, start:stop]).astype(BF16)

    def one_request(request, states):
        rows = phi_ref[request * span : (request + 1) * span, :]
        state = jnp.concatenate(states, axis=1) if local_heads > 1 else states[0]
        out = jnp.dot(rows, state, preferred_element_type=F32)
        for head in range(local_heads):
            at = head * slots
            history_ref[request * span + at : request * span + at + slots, :] = out[
                at : at + slots, head * head_size : (head + 1) * head_size
            ]

    request = 0
    for held_ref, many in zip(held_refs, held):
        for at in range(many):
            one_request(request, [held_ref[at, head] for head in range(local_heads)])
            request += 1
    if late:
        copy.wait()
        for at in range(requests - early):
            one_request(early + at, [late_ref[at, head] for head in range(local_heads)])

    for head in range(local_heads):
        logit = extra[:, head + 1 : head + 2] * inverse
        logit = logit + bias_ref[layer : layer + 1, head : head + 1]
        softplus = jnp.maximum(logit, 0.0) + jnp.log(1.0 + jnp.exp(-jnp.abs(logit)))
        decay = jnp.exp(-softplus)
        start = head * head_size
        key = pairs[:, start : start + head_size]
        value = pairs[:, start + kv_width : start + kv_width + head_size]
        for slot in range(group_size):
            start = (head * group_size + slot) * head_size
            query = queries[:, start : start + head_size]
            product = jnp.sum(query * key, axis=1, keepdims=True)
            cross = product * product / head_size
            part = decay * history_ref[pl.ds(head * slots + slot, requests, stride=span), :]
            part = part + cross * value
            own_ref[:, start : start + head_size] = part
            wire_ref[:, start : start + head_size] = part.astype(wire_ref.dtype)


def read(layer, sizes, wire, terms, gate_bias, picks, held, retained):
    local_heads, group_size, slots, head_size, _, _ = sizes
    requests = terms[0].shape[0]
    block_feat = picks[0].shape[1]
    width = local_heads * group_size * head_size
    counts = tuple(array.shape[0] for array in held)
    missing = requests - sum(counts)
    late = int(missing > 0)
    rows = requests * local_heads * slots
    return pl.pallas_call(
        functools.partial(read_kernel, layer, sizes, len(terms), counts, late),
        out_shape=[
            jax.ShapeDtypeStruct((requests, width), F32),
            jax.ShapeDtypeStruct((requests, width), wire),
        ],
        in_specs=[VMEM_SPEC] * (len(terms) + 4 + len(held)) + [HBM_SPEC] * late,
        out_specs=[VMEM_SPEC] * 2,
        scratch_shapes=[
            pltpu.VMEM((rows, head_size), F32),
            pltpu.VMEM((rows, block_feat), BF16),
            pltpu.VMEM((rows, head_size), F32),
        ]
        + [pltpu.VMEM((missing,) + retained.shape[2:], BF16), pltpu.SemaphoreType.DMA] * late,
        compiler_params=params(6 + 6 * late),
        name="read",
    )(
        *terms,
        gate_bias,
        *[resident(array) for array in (*picks, *held)],
        *[off_chip(retained)] * late,
    )


def mix_kernel(layer, count, held, *refs):
    terms = refs[:count]
    gain_ref, weight_ref = refs[count : count + 2]
    wire_ref, mixed_ref = refs[count + 2 + held :]
    head_size = gain_ref.shape[1]
    readout = add_terms(terms)
    gain = gain_ref[layer : layer + 1, :]
    for start in range(0, readout.shape[1], head_size):
        part = readout[:, start : start + head_size]
        mean = jnp.mean(part * part, axis=1, keepdims=True)
        mixed = part * lax.rsqrt(mean + EPS) * gain
        mixed_ref[:, start : start + head_size] = mixed.astype(BF16)
    out = jnp.dot(mixed_ref[...], weight_ref[layer], preferred_element_type=F32)
    wire_ref[...] = out.astype(wire_ref.dtype)


def mix(layer, wire, terms, read_gain, weight, held):
    requests, rows = terms[0].shape
    return pl.pallas_call(
        functools.partial(mix_kernel, layer, len(terms), len(held)),
        out_shape=jax.ShapeDtypeStruct((requests, weight.shape[2]), wire),
        in_specs=[VMEM_SPEC] * (len(terms) + 2) + [ANY_SPEC] * len(held),
        out_specs=VMEM_SPEC,
        scratch_shapes=[pltpu.VMEM((requests, rows), BF16)],
        compiler_params=params(8),
        name="mix",
    )(*terms, read_gain, resident(weight), *[resident(part) for part in held])


def finish_kernel(count, *refs):
    stream = refs[0][...].astype(F32) + add_terms(refs[1:count])
    refs[count][...] = stream.astype(BF16)


def finish(terms):
    return pl.pallas_call(
        functools.partial(finish_kernel, len(terms)),
        out_shape=jax.ShapeDtypeStruct(terms[0].shape, BF16),
        in_specs=[VMEM_SPEC] * len(terms),
        out_specs=VMEM_SPEC,
        compiler_params=params(2),
        name="finish",
    )(*terms)


def body(
    feat_size,
    head_ranks,
    token_ids,
    embedding,
    retained,
    query_weight,
    key_weight,
    value_weight,
    gate_weight,
    gate_bias,
    norm_gain,
    read_gain,
    out_weight,
):
    layer_count, requests, local_heads, block_feat, head_size = retained.shape
    group_size = query_weight.shape[2] // (local_heads * head_size)
    slots = -(-group_size // SUBLANES) * SUBLANES
    stream_width = norm_gain.shape[1]
    model_width = stream_width * feat_size
    sizes = (local_heads, group_size, slots, head_size, stream_width, model_width)
    feat_wire = wire_type(feat_size)
    head_wire = wire_type(head_ranks)
    weights = (query_weight, key_weight, value_weight)
    gate_rows = gate_weight.transpose(0, 2, 1)

    def fetch_state(layer, stage):
        shares = LATER_LAYER if layer else FIRST_LAYER
        start = requests * sum(shares[:stage]) // sum(shares)
        stop = requests * sum(shares[: stage + 1]) // sum(shares)
        if layer >= layer_count or start == stop:
            return []
        return list(fetch([retained], ((0, (layer, slice(start, stop))),)))

    picked, picks = pick_rows(token_ids, embedding, head_size, block_feat)
    stream_terms = exchange(picked, [picked], "head", head_ranks)
    carried, held = [], []
    for layer in range(layer_count):
        held = held + fetch_state(layer, 1)
        stream, own, wires = project(
            layer, carried, feat_size, stream_terms, norm_gain, weights, gate_rows, held
        )
        terms = exchange(own, wires, "feat", feat_size)
        held = held + fetch_state(layer, 2)
        own, wire = read(layer, sizes, feat_wire, terms, gate_bias, picks, held, retained)
        terms = exchange(own, [wire], "feat", feat_size)
        held = fetch_state(layer + 1, 0)
        wire = mix(layer, head_wire, terms, read_gain, out_weight, held)
        stream_terms = exchange(wire, [wire], "head", head_ranks)
        carried = [stream]
    return finish(carried + stream_terms)


def solution(mesh):
    return jax.shard_map(
        functools.partial(body, mesh.shape["feat"], mesh.shape["head"]),
        mesh=mesh,
        in_specs=(
            P("groups"),
            P("head", "feat"),
            P(None, "groups", "head", "feat", None),
            P(None, "feat", "head"),
            P(None, "feat", "head"),
            P(None, "feat", "head"),
            P(None, "feat", "head"),
            P(None, "head"),
            P(None, "feat"),
            P(),
            P(None, "head", "feat"),
        ),
        out_specs=P("groups", "feat"),
        check_vma=False,
    )
```

```python
import functools
import math

import jax
import jax.numpy as jnp
from jax import lax
from jax.experimental import pallas as pl
from jax.experimental.pallas import tpu as pltpu
from jax.sharding import PartitionSpec as P

EPS = 1e-6
LANES = 128
SUBLANES = 8
ROWS = 16
FIRST_LAYER = (0, 4, 8, 4)
LATER_LAYER = (5, 4, 7, 0)
MIB = 2**20
F32 = jnp.float32
BF16 = jnp.bfloat16

VMEM_SPEC = pl.BlockSpec(memory_space=pltpu.VMEM)
ANY_SPEC = pl.BlockSpec(memory_space=pl.ANY)
HBM_SPEC = pl.BlockSpec(memory_space=pltpu.HBM)
SMEM_SPEC = pl.BlockSpec(memory_space=pltpu.SMEM)


def params(mib):
    return pltpu.CompilerParams(vmem_limit_bytes=mib * MIB)


def resident(array):
    return pltpu.with_memory_space_constraint(array, pltpu.VMEM)


def off_chip(array):
    return pltpu.with_memory_space_constraint(array, pltpu.HBM)


def wire_type(size):
    return BF16 if size <= 4 else F32


def steps_of(size, axis):
    if size > 4:
        return ()
    order = (2, 3, 1) if axis == "feat" else (3, 2, 1)
    return tuple(step for step in order if step < size)


def exchange(own, wires, axis, size):
    steps = steps_of(size, axis)
    if not steps:
        (wire,) = wires
        return [own.astype(F32) - wire.astype(F32), lax.psum(wire.astype(F32), axis)]
    if len(wires) == 1:
        wires = wires * len(steps)
    return [own] + [
        lax.ppermute(wire, axis, [(rank, rank ^ step) for rank in range(size)])
        for wire, step in zip(wires, steps)
    ]


def own_rows(array, share, mine):
    rows = array[:share]
    for block in range(1, array.shape[0] // share):
        rows = jnp.where(mine == block, array[block * share : (block + 1) * share], rows)
    return rows


def split(wide):
    high = wide.astype(BF16)
    return high, (wide - high.astype(F32)).astype(BF16)


def split_dot(wide, weight):
    rows, depth = wide.shape
    empty = jnp.zeros((max(LANES - 2 * rows, 0), depth), BF16)
    parts = jnp.concatenate((*split(wide), empty), axis=0)
    out = jnp.dot(parts, weight, preferred_element_type=F32)
    return out[:rows] + out[rows : 2 * rows]


def add_terms(refs):
    terms = [ref[...].astype(F32) for ref in refs]
    while len(terms) > 1:
        terms = [sum(terms[at : at + 2]) for at in range(0, len(terms), 2)]
    return terms[0]


def make_selectors(left_ref, right_ref, scale_ref):
    size, block_feat = left_ref.shape

    def first_of(row):
        return row * size - row * (row - 1) // 2

    column = lax.broadcasted_iota(jnp.int32, (1, block_feat), 1)
    feature = lax.axis_index("feat") * block_feat + column
    reach = 2 * size + 1
    root = jnp.sqrt((reach * reach - 8 * feature).astype(F32))
    left = ((reach - root) * 0.5).astype(jnp.int32)
    left = jnp.where(first_of(left) > feature, left - 1, left)
    left = jnp.where(first_of(left + 1) <= feature, left + 1, left)
    right = feature - first_of(left) + left
    at = lax.broadcasted_iota(jnp.int32, left_ref.shape, 0)
    left_ref[...] = jnp.where(at == left, 1.0, 0.0).astype(BF16)
    right_ref[...] = jnp.where(at == right, 1.0, 0.0).astype(BF16)
    scale_ref[...] = jnp.where(left == right, 1.0, math.sqrt(2.0)).astype(F32)


def pick_kernel(ids_ref, table_ref, out_ref, left_ref, right_ref, scale_ref, groups_ref, sems):
    requests = out_ref.shape[0]
    table_rows = table_ref.shape[0]
    row_start = lax.axis_index("head") * table_rows
    row_at = lax.broadcasted_iota(jnp.int32, (requests, requests * ROWS), 0)
    column_at = lax.broadcasted_iota(jnp.int32, (requests, requests * ROWS), 1)
    chosen = jnp.zeros((requests, requests * ROWS), F32)
    groups_ref[...] = jnp.zeros_like(groups_ref)
    copies = []
    for request in range(requests):
        local_id = ids_ref[request] - row_start
        inside = (local_id >= 0) & (local_id < table_rows)
        row = jnp.clip(local_id, 0, table_rows - 1)
        first = pl.multiple_of((row // ROWS) * ROWS, ROWS)
        copy = pltpu.make_async_copy(
            table_ref.at[pl.ds(first, ROWS), :],
            groups_ref.at[pl.ds(request * ROWS, ROWS), :],
            sems.at[request],
        )
        pl.when(inside)(copy.start)
        copies.append((inside, copy))
        place = jnp.where(inside, request * ROWS + row - first, -1)
        chosen = jnp.where((row_at == request) & (column_at == place), 1.0, chosen)
    make_selectors(left_ref, right_ref, scale_ref)
    for inside, copy in copies:
        pl.when(inside)(copy.wait)
    out_ref[...] = jnp.dot(
        chosen.astype(BF16), groups_ref[...], preferred_element_type=F32
    ).astype(BF16)


def pick_rows(token_ids, embedding, head_size, block_feat):
    table_rows, width = embedding.shape
    requests = token_ids.shape[0]
    picks = [
        pltpu.VMEM((head_size, block_feat), BF16),
        pltpu.VMEM((head_size, block_feat), BF16),
        pltpu.VMEM((1, block_feat), F32),
    ]
    if table_rows % ROWS:
        picks = pl.pallas_call(
            make_selectors,
            out_shape=picks,
            out_specs=[VMEM_SPEC] * 3,
            compiler_params=params(8),
            name="selectors",
        )()
        local_ids = token_ids - lax.axis_index("head") * table_rows
        inside = (local_ids >= 0) & (local_ids < table_rows)
        picked = jnp.take(embedding, jnp.clip(local_ids, 0, table_rows - 1), axis=0)
        return jnp.where(inside[:, None], picked, jnp.zeros_like(picked)), picks
    picked, *picks = pl.pallas_call(
        pick_kernel,
        out_shape=[jax.ShapeDtypeStruct((requests, width), BF16)] + picks,
        in_specs=[SMEM_SPEC, HBM_SPEC],
        out_specs=[VMEM_SPEC] * 4,
        scratch_shapes=[
            pltpu.VMEM((requests * ROWS, width), BF16),
            pltpu.SemaphoreType.DMA((requests,)),
        ],
        compiler_params=params(8),
        name="pick_rows",
    )(off_chip(token_ids), off_chip(embedding))
    return picked, picks


def fetch_kernel(plan, count, *refs):
    sources, outs, sems = refs[:count], refs[count:-1], refs[-1]
    copies = []
    for at, (source, index) in enumerate(plan):
        copy = pltpu.make_async_copy(sources[source].at[index], outs[at], sems.at[at])
        copy.start()
        copies.append(copy)
    for copy in copies:
        copy.wait()


def fetch(sources, plan):
    shapes = []
    for source, index in plan:
        array = sources[source]
        index = index if isinstance(index, tuple) else (index,)
        shape = []
        for at, extent in enumerate(array.shape):
            if at >= len(index):
                shape.append(extent)
            elif isinstance(index[at], slice):
                shape.append(index[at].stop - index[at].start)
        shapes.append(pltpu.VMEM(tuple(shape), array.dtype))
    return pl.pallas_call(
        functools.partial(fetch_kernel, plan, len(sources)),
        out_shape=shapes,
        in_specs=[HBM_SPEC] * len(sources),
        out_specs=[VMEM_SPEC] * len(plan),
        scratch_shapes=[pltpu.SemaphoreType.DMA((len(plan),))],
        compiler_params=params(2),
        name="fetch",
    )(*[off_chip(source) for source in sources])


def project_kernel(layer, count, carried, held, steps, *refs):
    terms = refs[carried:count]
    gain_ref, query_ref, key_ref, value_ref, gate_ref = refs[count : count + 5]
    stream_ref, own_ref, *wire_refs = refs[count + 5 + held :]
    stream = add_terms(terms)
    if carried:
        stream = refs[0][...].astype(F32) + stream
    stream = stream.astype(BF16)
    stream_ref[...] = stream
    wide = stream.astype(F32)
    sum_sq = jnp.sum(wide * wide, axis=1, keepdims=True)
    scaled = wide * gain_ref[layer : layer + 1, :]
    parts = [
        split_dot(scaled, weight_ref[layer]) for weight_ref in (query_ref, key_ref, value_ref)
    ]
    requests = stream.shape[0]
    lane = lax.broadcasted_iota(jnp.int32, (requests, LANES), 1)
    half = LANES // 2
    place = jnp.where(lane >= half, lane - half, lane)
    extra = jnp.where(place == 0, sum_sq, 0.0)
    for head in range(gate_ref.shape[1]):
        column = gate_ref[layer, head : head + 1, :].astype(F32)
        gate = jnp.sum(scaled * column, axis=1, keepdims=True)
        extra = jnp.where(place == head + 1, gate, extra)
    rounded = extra.astype(BF16).astype(F32)
    sent = jnp.where(lane < half, rounded, extra - rounded)
    kept = jnp.where(lane < half, extra, 0.0)
    start = 0
    for part, other in zip((parts[0], kept, *parts[1:]), (parts[0], sent, *parts[1:])):
        stop = start + part.shape[1]
        own_ref[:, start:stop] = part
        for wire_ref in wire_refs:
            if stop <= wire_ref.shape[1]:
                wire_ref[:, start:stop] = other.astype(wire_ref.dtype)
        start = stop
    for step, wire_ref in zip(steps, wire_refs):
        share = requests // (len(steps) + 1)
        partner = lax.axis_index("feat") ^ step
        packed = [
            own_rows(part[:, at : at + LANES], share, partner)
            for part in parts[1:]
            for at in range(0, part.shape[1], LANES)
        ]
        wire_ref[:, -LANES:] = jnp.concatenate(packed, axis=0).astype(wire_ref.dtype)


def packs(requests, weights, size):
    blocks = sum(weight.shape[2] for weight in weights[1:]) // LANES
    return len(steps_of(size, "feat")) > 0 and blocks == size and requests % size == 0


def project(layer, carried, size, terms, norm_gain, weights, gate_weight, held):
    terms = carried + terms
    requests, width = terms[0].shape
    query_width = weights[0].shape[2]
    total = sum(weight.shape[2] for weight in weights) + LANES
    if packs(requests, weights, size):
        steps, sent = steps_of(size, "feat"), query_width + 2 * LANES
    else:
        steps, sent = (), total
    wires = [jax.ShapeDtypeStruct((requests, sent), wire_type(size))] * max(len(steps), 1)
    stream, own, *wires = pl.pallas_call(
        functools.partial(project_kernel, layer, len(terms), len(carried), len(held), steps),
        out_shape=[
            jax.ShapeDtypeStruct((requests, width), BF16),
            jax.ShapeDtypeStruct((requests, total), F32),
        ]
        + wires,
        in_specs=[VMEM_SPEC] * (len(terms) + 5) + [ANY_SPEC] * len(held),
        out_specs=[VMEM_SPEC] * (2 + len(wires)),
        compiler_params=params(8),
        name="project",
    )(
        *terms,
        norm_gain,
        *[resident(weight) for weight in weights],
        gate_weight,
        *[resident(part) for part in held],
    )
    return stream, own, wires


def read_kernel(layer, sizes, count, held, late, *refs):
    local_heads, group_size, slots, head_size, stream_width, model_width = sizes
    terms = refs[:count]
    bias_ref, left_ref, right_ref, scale_ref = refs[count : count + 4]
    held_refs = refs[count + 4 : count + 4 + len(held)]
    rest = refs[count + 4 + len(held) :]
    own_ref, wire_ref, rows_ref, phi_ref, history_ref = rest[late:][:5]
    requests = own_ref.shape[0]
    block_feat = phi_ref.shape[1]
    if late:
        state_ref, late_ref, sem = rest[0], *rest[-2:]
        early = sum(held)
        copy = pltpu.make_async_copy(
            state_ref.at[layer, early:requests], late_ref.at[: requests - early], sem
        )
        copy.start()
    query_width = local_heads * group_size * head_size
    kv_width = local_heads * head_size
    own, others = terms[0], terms[1:]
    common = query_width + LANES
    total = add_terms([ref.at[:, :common] for ref in terms])
    extra = total[:, query_width:]
    half = LANES // 2
    extra = extra[:, :half] + extra[:, half:]
    inverse = lax.rsqrt(extra[:, 0:1] / model_width + EPS)
    queries = total[:, :query_width] * inverse

    feat_size = model_width // stream_width
    share = requests // feat_size
    mine = lax.axis_index("feat")
    if others[0].shape[1] == own.shape[1]:
        pairs = add_terms([ref.at[:, common:] for ref in terms])
        pairs = own_rows(pairs, share, mine)
    else:
        packed = add_terms([ref.at[:, common:] for ref in others])
        pairs = own_rows(own[:, common:], share, mine) + jnp.concatenate(
            [packed[at : at + share] for at in range(0, requests, share)], axis=1
        )
    pairs = jnp.concatenate([pairs] * feat_size, axis=0) * inverse
    block = lax.broadcasted_iota(jnp.int32, (requests, 1), 0) // share
    pairs = jnp.where(block == mine, pairs, 0.0)

    span = local_heads * slots
    for head in range(local_heads):
        for slot in range(slots):
            if slot < group_size:
                start = (head * group_size + slot) * head_size
                part = queries[:, start : start + head_size]
            else:
                part = jnp.zeros((requests, head_size), F32)
            rows_ref[pl.ds(head * slots + slot, requests, stride=span), :] = part
    vectors = rows_ref[...].astype(BF16)

    step = 2 * LANES
    for start in range(0, block_feat, step):
        stop = min(start + step, block_feat)
        left = jnp.dot(vectors, left_ref[:, start:stop], preferred_element_type=F32)
        right = jnp.dot(vectors, right_ref[:, start:stop], preferred_element_type=F32)
        phi_ref[:, start:stop] = (left * right * scale_ref[:, start:stop]).astype(BF16)

    def one_request(request, states):
        rows = phi_ref[request * span : (request + 1) * span, :]
        state = jnp.concatenate(states, axis=1) if local_heads > 1 else states[0]
        out = jnp.dot(rows, state, preferred_element_type=F32)
        for head in range(local_heads):
            at = head * slots
            history_ref[request * span + at : request * span + at + slots, :] = out[
                at : at + slots, head * head_size : (head + 1) * head_size
            ]

    request = 0
    for held_ref, many in zip(held_refs, held):
        for at in range(many):
            one_request(request, [held_ref[at, head] for head in range(local_heads)])
            request += 1
    if late:
        copy.wait()
        for at in range(requests - early):
            one_request(early + at, [late_ref[at, head] for head in range(local_heads)])

    for head in range(local_heads):
        logit = extra[:, head + 1 : head + 2] * inverse
        logit = logit + bias_ref[layer : layer + 1, head : head + 1]
        softplus = jnp.maximum(logit, 0.0) + jnp.log(1.0 + jnp.exp(-jnp.abs(logit)))
        decay = jnp.exp(-softplus)
        start = head * head_size
        key = pairs[:, start : start + head_size]
        value = pairs[:, start + kv_width : start + kv_width + head_size]
        for slot in range(group_size):
            start = (head * group_size + slot) * head_size
            query = queries[:, start : start + head_size]
            product = jnp.sum(query * key, axis=1, keepdims=True)
            cross = product * product / head_size
            part = decay * history_ref[pl.ds(head * slots + slot, requests, stride=span), :]
            part = part + cross * value
            own_ref[:, start : start + head_size] = part
            wire_ref[:, start : start + head_size] = part.astype(wire_ref.dtype)


def read(layer, sizes, wire, terms, gate_bias, picks, held, retained):
    local_heads, group_size, slots, head_size, _, _ = sizes
    requests = terms[0].shape[0]
    block_feat = picks[0].shape[1]
    width = local_heads * group_size * head_size
    counts = tuple(array.shape[0] for array in held)
    missing = requests - sum(counts)
    late = int(missing > 0)
    rows = requests * local_heads * slots
    return pl.pallas_call(
        functools.partial(read_kernel, layer, sizes, len(terms), counts, late),
        out_shape=[
            jax.ShapeDtypeStruct((requests, width), F32),
            jax.ShapeDtypeStruct((requests, width), wire),
        ],
        in_specs=[VMEM_SPEC] * (len(terms) + 4 + len(held)) + [HBM_SPEC] * late,
        out_specs=[VMEM_SPEC] * 2,
        scratch_shapes=[
            pltpu.VMEM((rows, head_size), F32),
            pltpu.VMEM((rows, block_feat), BF16),
            pltpu.VMEM((rows, head_size), F32),
        ]
        + [pltpu.VMEM((missing,) + retained.shape[2:], BF16), pltpu.SemaphoreType.DMA] * late,
        compiler_params=params(6 + 6 * late),
        name="read",
    )(
        *terms,
        gate_bias,
        *[resident(array) for array in (*picks, *held)],
        *[off_chip(retained)] * late,
    )


def mix_kernel(layer, count, held, *refs):
    terms = refs[:count]
    gain_ref, weight_ref = refs[count : count + 2]
    wire_ref, mixed_ref = refs[count + 2 + held :]
    head_size = gain_ref.shape[1]
    readout = add_terms(terms)
    gain = gain_ref[layer : layer + 1, :]
    for start in range(0, readout.shape[1], head_size):
        part = readout[:, start : start + head_size]
        mean = jnp.mean(part * part, axis=1, keepdims=True)
        mixed = part * lax.rsqrt(mean + EPS) * gain
        mixed_ref[:, start : start + head_size] = mixed.astype(BF16)
    out = jnp.dot(mixed_ref[...], weight_ref[layer], preferred_element_type=F32)
    wire_ref[...] = out.astype(wire_ref.dtype)


def mix(layer, wire, terms, read_gain, weight, held):
    requests, rows = terms[0].shape
    return pl.pallas_call(
        functools.partial(mix_kernel, layer, len(terms), len(held)),
        out_shape=jax.ShapeDtypeStruct((requests, weight.shape[2]), wire),
        in_specs=[VMEM_SPEC] * (len(terms) + 2) + [ANY_SPEC] * len(held),
        out_specs=VMEM_SPEC,
        scratch_shapes=[pltpu.VMEM((requests, rows), BF16)],
        compiler_params=params(8),
        name="mix",
    )(*terms, read_gain, resident(weight), *[resident(part) for part in held])


def finish_kernel(count, *refs):
    stream = refs[0][...].astype(F32) + add_terms(refs[1:count])
    refs[count][...] = stream.astype(BF16)


def finish(terms):
    return pl.pallas_call(
        functools.partial(finish_kernel, len(terms)),
        out_shape=jax.ShapeDtypeStruct(terms[0].shape, BF16),
        in_specs=[VMEM_SPEC] * len(terms),
        out_specs=VMEM_SPEC,
        compiler_params=params(2),
        name="finish",
    )(*terms)


def body(
    feat_size,
    head_ranks,
    token_ids,
    embedding,
    retained,
    query_weight,
    key_weight,
    value_weight,
    gate_weight,
    gate_bias,
    norm_gain,
    read_gain,
    out_weight,
):
    layer_count, requests, local_heads, block_feat, head_size = retained.shape
    group_size = query_weight.shape[2] // (local_heads * head_size)
    slots = -(-group_size // SUBLANES) * SUBLANES
    stream_width = norm_gain.shape[1]
    model_width = stream_width * feat_size
    sizes = (local_heads, group_size, slots, head_size, stream_width, model_width)
    feat_wire = wire_type(feat_size)
    head_wire = wire_type(head_ranks)
    weights = (query_weight, key_weight, value_weight)
    gate_rows = gate_weight.transpose(0, 2, 1)

    def fetch_state(layer, stage):
        shares = LATER_LAYER if layer else FIRST_LAYER
        start = requests * sum(shares[:stage]) // sum(shares)
        stop = requests * sum(shares[: stage + 1]) // sum(shares)
        if layer >= layer_count or start == stop:
            return []
        return list(fetch([retained], ((0, (layer, slice(start, stop))),)))

    picked, picks = pick_rows(token_ids, embedding, head_size, block_feat)
    stream_terms = exchange(picked, [picked], "head", head_ranks)
    carried, held = [], []
    for layer in range(layer_count):
        held = held + fetch_state(layer, 1)
        stream, own, wires = project(
            layer, carried, feat_size, stream_terms, norm_gain, weights, gate_rows, held
        )
        terms = exchange(own, wires, "feat", feat_size)
        held = held + fetch_state(layer, 2)
        own, wire = read(layer, sizes, feat_wire, terms, gate_bias, picks, held, retained)
        terms = exchange(own, [wire], "feat", feat_size)
        held = fetch_state(layer + 1, 0)
        wire = mix(layer, head_wire, terms, read_gain, out_weight, held)
        stream_terms = exchange(wire, [wire], "head", head_ranks)
        carried = [stream]
    return finish(carried + stream_terms)


def solution(mesh):
    return jax.shard_map(
        functools.partial(body, mesh.shape["feat"], mesh.shape["head"]),
        mesh=mesh,
        in_specs=(
            P("groups"),
            P("head", "feat"),
            P(None, "groups", "head", "feat", None),
            P(None, "feat", "head"),
            P(None, "feat", "head"),
            P(None, "feat", "head"),
            P(None, "feat", "head"),
            P(None, "head"),
            P(None, "feat"),
            P(),
            P(None, "head", "feat"),
        ),
        out_specs=P("groups", "feat"),
        check_vma=False,
    )
```
